512 devices in a mesh: scen: 16 (over y, core), fac: 32 (over z, x).
Axes of the slice: x: 4, y: 8, z: 8, core: 2. Of those that a mesh axis runs over, the one named last changes fastest.
Arguments:
- shocks: bfloat16 [2, 4096, 256], P(None, 'scen'), may hold values from -6 to 6
- loadings: bfloat16 [256, 8192], P(None, 'fac'), may hold values from -0.375 to 0.375
- vol: float32 [8192], P('fac'), may hold values from 0.1 to 0.5
- jump_counts: int32 [2, 4096, 8192], P(None, 'scen', 'fac'), may hold values from 0 to 3
- jump_noise: bfloat16 [2, 4096, 8192], P(None, 'scen', 'fac'), may hold values from -6 to 6
- jump_mean: float32 [8192], P('fac'), may hold values from -0.15 to 0.1
- jump_vol: float32 [8192], P('fac'), may hold values from 0.05 to 0.3
- dependencies: int32 [8192, 2], P('fac'), may hold values from 0 to 63, as said below
- block_slot: int32 [64], replicated, may hold values from 0 to 63, each once
- trade_weights: bfloat16 [8192, 2, 128], P('fac'), may hold values from -0.375 to 0.375
- netting: int32 [8192], P('fac'), may hold values from 0 to 2047
Outputs:
- exposure: float32 [2, 2048, 4096], P(None, 'fac', 'scen')
- expected: float32 [2, 2048], P(None, 'fac')
The draws below stay inside these ranges and needn't reach their ends.
Inputs may be any that keep to these rules, and one draw needn't show every extreme that they name: `dependencies`: each trade names 2 different blocks.
All inputs are finite; a program needn't handle non-finite values.
Results may differ from the reference program's by a relative error of at most 0.0056.
Values may be sent and summed in bfloat16 or wider, within the bound.
A program may use at most 192 MiB of HBM per device.

```python
import math
import jax
import jax.numpy as jnp
from jax import lax

SHOCKS = 256
BLOCK = 128
DEPS = 2
DATES = 2
SCENARIOS = 4096
FACTORS = 8192
NBLOCKS = 64
TRADES = 8192
NSETS = 2048


def draw_dependencies(key, part):
    key = jax.random.fold_in(key, 11)
    heat_key, score_key = jax.random.split(key)
    heat = jax.random.randint(heat_key, (NBLOCKS,), 0, 4)
    scores = jax.random.randint(score_key, (TRADES, NBLOCKS), 0, 65536) + heat[None, :] * 16384
    scores = scores * NBLOCKS + jnp.arange(NBLOCKS, dtype=jnp.int32)[None, :]
    return lax.top_k(scores, DEPS)[1].astype(jnp.int32)


def plant(values, stream_key, low, high):
    place = [jax.random.randint(jax.random.fold_in(stream_key, axis), (), 0, length) for axis, length in enumerate(values.shape)]
    widest = values.shape.index(max(values.shape))
    beside = place[:widest] + [(place[widest] + 1) % values.shape[widest]] + place[widest + 1:]
    return values.at[tuple(place)].set(low).at[tuple(beside)].set(high)


def block_levels(key, dims, pieces, least, high):
    def one(axis_at, shards_of):
        heights = jax.random.uniform(jax.random.fold_in(jax.random.fold_in(key, 6), axis_at), (shards_of,), jnp.float32, least / len(pieces), high / len(pieces))
        return jnp.repeat(jnp.exp(heights), dims[axis_at] // shards_of).reshape((-1,) + (1,) * (len(dims) - axis_at - 1))

    factor_of = one(*pieces[0])
    for cut in pieces[1:]:
        factor_of = factor_of * one(*cut)
    return factor_of


def gaussian(rng, shape, width, most, cuts=(), kind=jnp.bfloat16):
    values = width * jax.random.normal(rng, shape, jnp.float32)
    if cuts:
        values = values * block_levels(rng, shape, cuts, -0.22, 0.18)
    return jnp.clip(values, -most, most).astype(kind)


def setup_inputs(seed: int = 0) -> dict:
    arg_keys = jax.random.split(jax.random.key(seed), 12)
    shocks = gaussian(arg_keys[0], (DATES, SCENARIOS, SHOCKS), 1.0, 6.0, ((1, 16),))
    loadings = gaussian(arg_keys[1], (SHOCKS, FACTORS), SHOCKS ** -0.5, 0.375, ((1, 32),))
    vol = jnp.clip(jnp.exp(math.log(0.5) - 1.609438 * jax.random.uniform(arg_keys[2], (FACTORS,), jnp.float32) ** block_levels(arg_keys[2], (FACTORS,), ((0, 32),), -0.2, 0.2)), 0.1, 0.5)
    jump_counts = plant(jax.random.randint(arg_keys[3], (DATES, SCENARIOS, FACTORS), 0, 4), jax.random.fold_in(arg_keys[3], 1), 0, 3).astype(jnp.int32)
    jump_noise = gaussian(arg_keys[4], (DATES, SCENARIOS, FACTORS), 1.0, 6.0, ((1, 16), (2, 32)))
    jump_mean = jnp.clip(-0.15 + 0.25 * jax.random.uniform(arg_keys[5], (FACTORS,), jnp.float32) ** block_levels(arg_keys[5], (FACTORS,), ((0, 32),), -0.2, 0.2), -0.15, 0.1)
    jump_vol = jnp.clip(jnp.exp(math.log(0.3) - 1.7917595 * jax.random.uniform(arg_keys[6], (FACTORS,), jnp.float32) ** block_levels(arg_keys[6], (FACTORS,), ((0, 32),), -0.2, 0.2)), 0.05, 0.3)
    dependencies = draw_dependencies(jax.random.fold_in(arg_keys[11], 71), 0)
    block_slot = jax.random.permutation(arg_keys[8], NBLOCKS).astype(jnp.int32)
    trade_weights = gaussian(arg_keys[9], (TRADES, DEPS, BLOCK), (DEPS * BLOCK) ** -0.5, 0.375, ((0, 32),))
    netting = plant(jax.random.randint(arg_keys[10], (TRADES,), 0, NSETS), jax.random.fold_in(arg_keys[10], 1), 0, NSETS - 1).astype(jnp.int32)
    return dict(shocks=shocks, loadings=loadings, vol=vol, jump_counts=jump_counts, jump_noise=jump_noise, jump_mean=jump_mean, jump_vol=jump_vol, dependencies=dependencies, block_slot=block_slot, trade_weights=trade_weights, netting=netting)


def price_trades(blocks, slots, weights):

    def one(part):
        total = jnp.zeros((part.shape[0], slots.shape[0]), jnp.float32)
        for k in range(DEPS):
            chosen = part[:, slots[:, k], :].astype(jnp.float32)
            total = total + jnp.einsum('stj,tj->st', chosen, weights[:, k, :].astype(jnp.float32))
        return total
    grouped = blocks.reshape(SCENARIOS // 32, 32, NBLOCKS, BLOCK)
    return lax.map(one, grouped).reshape(SCENARIOS, TRADES)

def reference(shocks, loadings, vol, jump_counts, jump_noise, jump_mean, jump_vol, dependencies, block_slot, trade_weights, netting):
    level = jnp.zeros((SCENARIOS, FACTORS), jnp.float32)
    slots = block_slot[dependencies]
    exposures = []
    expects = []
    for date in range(DATES):
        diffuse = jnp.dot(shocks[date], loadings, preferred_element_type=jnp.float32)
        counts = jump_counts[date].astype(jnp.float32)
        level = level + vol * diffuse - 0.5 * vol * vol + counts * jump_mean + jnp.sqrt(counts) * jump_vol * jump_noise[date].astype(jnp.float32)
        prices = (jnp.exp(level) - 1.0).astype(jnp.bfloat16)
        values = price_trades(prices.reshape(SCENARIOS, NBLOCKS, BLOCK), slots, trade_weights)
        nets = jax.ops.segment_sum(values.T, netting, num_segments=NSETS)
        exposure = jnp.maximum(nets, 0.0)
        exposures.append(exposure)
        expects.append(lax.optimization_barrier(jnp.sum(exposure, axis=1)) / SCENARIOS)
    return (jnp.stack(exposures), jnp.stack(expects))
```

```python
import functools

import jax
import jax.numpy as jnp
from jax import lax
from jax.experimental import pallas as pl
from jax.experimental.pallas import tpu as pltpu
from jax.sharding import PartitionSpec as P

BLOCK = 128
SETS = 64
DATES = 2
CORES = 2
XS = 4
MESH = pl.DeviceIdType.MESH
F32 = jnp.float32
BF16 = jnp.bfloat16
NT = (((1,), (1,)), ((), ()))


class Ring:
    def __init__(self, n, me, axis, device, view, send, recv):
        self.n, self.me, self.axis, self.device, self.view = n, me, axis, device, view
        self.send, self.recv = send, recv
        self.last = n // 2

    def ref(self, way, d, owner):
        half = None
        if d == self.last:
            half = 0 if way == 0 else 1
        return self.view(owner, half)

    def owner(self, way, d):
        step = -d if way == 0 else d
        return lax.rem(self.me + step + self.n, self.n)

    def copy(self, way, d, shift):
        ref = self.ref(way, d, self.owner(way, d - shift))
        to = self.owner(way, -1)
        return pltpu.make_async_remote_copy(
            src_ref=ref,
            dst_ref=ref,
            send_sem=self.send.at[way, d],
            recv_sem=self.recv.at[way, d],
            device_id={self.axis: self.device(to)},
            device_id_type=MESH,
        )

    def start(self, way, d):
        self.copy(way, d, 1).start()

    def arrived(self, way, d):
        self.copy(way, d, 0).wait_recv()

    def sent(self):
        for d in range(1, self.last + 1):
            for way in range(2):
                self.copy(way, d, 1).wait_send()


def kernel(
    fac_n,
    scen_n,
    shocks,
    loadings,
    vol,
    counts,
    noise,
    jump_mean,
    jump_vol,
    deps,
    place,
    weights,
    netting,
    expo,
    mean,
    w32,
    keys,
    wg,
    marks,
    spread,
    macc,
    mg,
    level,
    pg,
    nets,
    part,
    back,
    sums,
    z_send,
    z_recv,
    x_send,
    x_recv,
    p_send,
    p_recv,
    m_send,
    m_recv,
    c_send,
    c_recv,
    r_send,
    r_recv,
    s_send,
    s_recv,
):
    zs = fac_n // XS
    ys = scen_n // CORES
    rows = shocks.shape[1]
    width = loadings.shape[1]
    local = width // BLOCK
    trades = netting.shape[1]
    jn = BLOCK // scen_n
    blocks = XS * local
    fac = lax.axis_index("fac")
    scen = lax.axis_index("scen")
    z, x = fac // XS, lax.rem(fac, XS)
    y, c = scen // CORES, lax.rem(scen, CORES)

    dep = deps[...]
    slot = jnp.zeros_like(dep)
    for b in range(place.shape[0]):
        slot = jnp.where(dep == b, place[b], slot)
    keys[x, z, :, 0:trades] = slot[0:1]
    keys[x, z, :, trades : 2 * trades] = slot[1:2]
    keys[x, z, :, 2 * trades : 3 * trades] = netting[...]
    w32[...] = weights[...].astype(F32)
    pick = (
        lax.broadcasted_iota(jnp.int32, (jn, BLOCK), 1)
        == lax.broadcasted_iota(jnp.int32, (jn, BLOCK), 0) + scen * jn
    ).astype(F32).astype(BF16)
    chosen = [
        lax.dot_general(
            pick, w32[pl.ds(k, trades, stride=2), :].astype(BF16), NT, preferred_element_type=F32
        )
        for k in range(2)
    ]
    wg[x, z] = jnp.concatenate(chosen, axis=0).astype(BF16)

    barrier = pltpu.get_barrier_semaphore()
    partners = 0
    for d in range(1, zs):
        pl.semaphore_signal(
            barrier, inc=1, device_id={"fac": lax.rem(z + d, zs) * XS + x}, device_id_type=MESH
        )
        partners += 1
    for d in range(1, XS):
        pl.semaphore_signal(
            barrier, inc=1, device_id={"fac": z * XS + lax.rem(x + d, XS)}, device_id_type=MESH
        )
        partners += 1
    for d in range(1, scen_n):
        pl.semaphore_signal(
            barrier, inc=1, device_id={"scen": lax.rem(scen + d, scen_n)}, device_id_type=MESH
        )
        partners += 1
    pl.semaphore_wait(barrier, partners)

    def z_copy(kind, d, from_z):
        ref = keys.at[x, from_z] if kind == 0 else wg.at[x, from_z]
        return pltpu.make_async_remote_copy(
            src_ref=ref,
            dst_ref=ref,
            send_sem=z_send.at[kind, d],
            recv_sem=z_recv.at[kind, d],
            device_id={"fac": lax.rem(z + d, zs) * XS + x},
            device_id_type=MESH,
        )

    def x_copy(kind, d, from_x):
        ref = keys.at[from_x] if kind == 0 else wg.at[from_x]
        return pltpu.make_async_remote_copy(
            src_ref=ref,
            dst_ref=ref,
            send_sem=x_send.at[kind, d],
            recv_sem=x_recv.at[kind, d],
            device_id={"fac": z * XS + lax.rem(x + d, XS)},
            device_id_type=MESH,
        )

    for kind in range(2):
        for d in range(1, zs):
            z_copy(kind, d, z).start()

    col_q = lax.broadcasted_iota(jnp.int32, (width, width), 1)
    col_f = (
        lax.rem(lax.div(col_q, jn), local) * BLOCK
        + lax.div(col_q, jn * local) * jn
        + lax.rem(col_q, jn)
    )
    perm = (lax.broadcasted_iota(jnp.int32, (width, width), 0) == col_f).astype(F32).astype(BF16)
    v = vol[...]
    drift = 0.5 * v * v
    for date in range(DATES):
        diffuse = jnp.dot(shocks[date], loadings[...], preferred_element_type=F32)
        number = counts[date].astype(F32)
        change = (
            v * diffuse
            - drift
            + number * jump_mean[...]
            + jnp.sqrt(number) * jump_vol[...] * noise[date].astype(F32)
        )
        now = change if date == 0 else level[...] + change
        if date < DATES - 1:
            level[...] = now
        prices = (jnp.exp(now) - 1.0).astype(BF16)
        pg[date, x] = jnp.dot(prices, perm, preferred_element_type=F32).astype(BF16)

    p_rings = []
    for date in range(DATES):

        def p_view(owner, half, date=date):
            if half is None:
                return pg.at[date, owner]
            return pg.at[date, owner, pl.ds(half * (rows // 2), rows // 2)]

        p_rings.append(
            Ring(XS, x, "fac", lambda i: z * XS + i, p_view, p_send.at[date], p_recv.at[date])
        )

    for kind in range(2):
        for d in range(1, zs):
            z_copy(kind, d, lax.rem(z - d + zs, zs)).wait_recv()
    for kind in range(2):
        for d in (1, XS - 1, 2):
            x_copy(kind, d, x).start()
    for ring in p_rings:
        for way in range(2):
            ring.start(way, 1)

    sets = zs * SETS
    macc[...] = jnp.zeros_like(macc)

    def form(owner):
        @pl.loop(0, zs)
        def _(at):
            columns = pl.ds(pl.multiple_of(at * trades, trades), trades)
            key = keys[owner, at]
            net = key[:, 2 * trades : 3 * trades]
            group = lax.shift_right_logical(net, 6)
            line = jnp.where(
                (group & (XS - 1)) == x,
                lax.shift_right_logical(group, 2) * SETS + (net & (SETS - 1)),
                -1,
            )
            marks[:, columns] = jnp.where(
                lax.broadcasted_iota(jnp.int32, (sets, trades), 0) == line, 1.0, 0.0
            ).astype(BF16)
            w = wg[owner, at].astype(F32)
            w0, w1 = w[0:jn], w[jn : 2 * jn]
            first = key[:, 0:trades] - blocks * z
            second = key[:, trades : 2 * trades] - blocks * z
            spread[:, columns] = jnp.concatenate(
                [
                    jnp.where(first == b, w0, 0.0) + jnp.where(second == b, w1, 0.0)
                    for b in range(blocks)
                ],
                axis=0,
            ).astype(BF16)

        macc[...] += lax.dot_general(spread[...], marks[...], NT, preferred_element_type=F32)

    form(x)
    for d in (1, XS - 1, 2):
        from_x = lax.rem(x - d + XS, XS)
        for kind in range(2):
            x_copy(kind, d, from_x).wait_recv()
        form(from_x)
    mg[scen] = macc[...].astype(BF16)

    half_rows = macc.shape[0] // 2

    def m_view(core):
        def view(owner, half):
            if half is None:
                return mg.at[owner * CORES + core]
            return mg.at[owner * CORES + core, pl.ds(half * half_rows, half_rows)]

        return view

    m_ring = Ring(ys, y, "scen", lambda i: i * CORES + c, m_view(c), m_send, m_recv)
    other = 1 - c

    def c_copy(way, d, mine):
        if d == 0:
            ref = m_view(c if mine else other)(y, None)
        else:
            half = None if d < m_ring.last else way
            ref = m_view(c if mine else other)(m_ring.owner(way, d), half)
        return pltpu.make_async_remote_copy(
            src_ref=ref,
            dst_ref=ref,
            send_sem=c_send.at[way, d],
            recv_sem=c_recv.at[way, d],
            device_id={"scen": y * CORES + other},
            device_id_type=MESH,
        )

    for way in range(2):
        m_ring.start(way, 1)
    c_copy(0, 0, True).start()
    for d in range(1, XS // 2):
        for ring in p_rings:
            for way in range(2):
                ring.arrived(way, d)
                ring.start(way, d + 1)
    for d in range(1, ys // 2 + 1):
        for way in range(2):
            m_ring.arrived(way, d)
            if d < ys // 2:
                m_ring.start(way, d + 1)
            c_copy(way, d, True).start()
    for ring in p_rings:
        for way in range(2):
            ring.arrived(way, XS // 2)
    c_copy(0, 0, False).wait_recv()
    for d in range(1, ys // 2 + 1):
        for way in range(2):
            c_copy(way, d, False).wait_recv()

    def r_copy(date, d, slot_at):
        return pltpu.make_async_remote_copy(
            src_ref=part.at[date, slot_at],
            dst_ref=back.at[date, d],
            send_sem=r_send.at[date, d],
            recv_sem=r_recv.at[date, d],
            device_id={"fac": lax.rem(z + d, zs) * XS + x},
            device_id_type=MESH,
        )

    tall = local * jn
    for date in range(DATES):
        total = None
        for at in range(XS):
            term = jnp.dot(
                pg[date, at],
                mg[:, at * tall : (at + 1) * tall, :].reshape(scen_n * tall, sets),
                preferred_element_type=F32,
            )
            total = term if total is None else total + term
        turned = total.T.reshape(zs, SETS, rows)
        nets[date] = turned
        part[date] = turned.astype(BF16)
        for d in range(1, zs):
            r_copy(date, d, lax.rem(z + d, zs)).start()
    for date in range(DATES):
        total = nets[date, z]
        for d in range(1, zs):
            r_copy(date, d, 0).wait_recv()
            total = total + back[date, d].astype(F32)
        expo[date] = jnp.maximum(total, 0.0)

    both = jnp.concatenate([expo[date] for date in range(DATES)], axis=0)
    ones = jnp.ones((8, rows), F32)
    row = lax.dot_general(
        ones, both, NT, precision=lax.Precision.HIGHEST, preferred_element_type=F32
    )
    sums[0] = row[0:1]

    def s_copy(d):
        return pltpu.make_async_remote_copy(
            src_ref=sums.at[0],
            dst_ref=sums.at[d],
            send_sem=s_send.at[d],
            recv_sem=s_recv.at[d],
            device_id={"scen": lax.rem(scen + d, scen_n)},
            device_id_type=MESH,
        )

    for d in range(1, scen_n):
        s_copy(d).start()
    for d in range(1, scen_n):
        s_copy(d).wait_recv()
    average = jnp.sum(sums[...], axis=0) / (rows * scen_n)
    for date in range(DATES):
        mean[date : date + 1, :] = average[:, date * SETS : (date + 1) * SETS]

    for kind in range(2):
        for d in range(1, zs):
            z_copy(kind, d, z).wait_send()
        for d in range(1, XS):
            x_copy(kind, d, x).wait_send()
    for ring in p_rings:
        ring.sent()
    m_ring.sent()
    c_copy(0, 0, True).wait_send()
    for d in range(1, ys // 2 + 1):
        for way in range(2):
            c_copy(way, d, True).wait_send()
    for date in range(DATES):
        for d in range(1, zs):
            r_copy(date, d, 0).wait_send()
    for d in range(1, scen_n):
        s_copy(d).wait_send()


def body(
    shocks,
    loadings,
    vol,
    jump_counts,
    jump_noise,
    jump_mean,
    jump_vol,
    dependencies,
    block_slot,
    trade_weights,
    netting,
):
    fac_n = lax.axis_size("fac")
    scen_n = lax.axis_size("scen")
    zs = fac_n // XS
    ys = scen_n // CORES
    rows = shocks.shape[1]
    width = loadings.shape[1]
    trades = netting.shape[0]
    local = width // BLOCK
    jn = BLOCK // scen_n
    tall = XS * local * jn
    sets = zs * SETS
    vmem = pl.BlockSpec(memory_space=pltpu.VMEM)
    smem = pl.BlockSpec(memory_space=pltpu.SMEM)
    dma = pltpu.SemaphoreType.DMA
    return pl.pallas_call(
        functools.partial(kernel, fac_n, scen_n),
        out_shape=(
            jax.ShapeDtypeStruct((DATES, SETS, rows), F32),
            jax.ShapeDtypeStruct((DATES, SETS), F32),
        ),
        in_specs=[vmem] * 8 + [smem] + [vmem] * 2,
        out_specs=(vmem, vmem),
        scratch_shapes=[
            pltpu.VMEM((2 * trades, BLOCK), F32),
            pltpu.VMEM((XS, zs, 1, 3 * trades), jnp.int32),
            pltpu.VMEM((XS, zs, 2 * jn, trades), BF16),
            pltpu.VMEM((sets, zs * trades), BF16),
            pltpu.VMEM((tall, zs * trades), BF16),
            pltpu.VMEM((tall, sets), F32),
            pltpu.VMEM((scen_n, tall, sets), BF16),
            pltpu.VMEM((rows, width), F32),
            pltpu.VMEM((DATES, XS, rows, width), BF16),
            pltpu.VMEM((DATES, zs, SETS, rows), F32),
            pltpu.VMEM((DATES, zs, SETS, rows), BF16),
            pltpu.VMEM((DATES, zs, SETS, rows), BF16),
            pltpu.VMEM((scen_n, 1, DATES * SETS), F32),
            dma((2, zs)),
            dma((2, zs)),
            dma((2, XS)),
            dma((2, XS)),
            dma((DATES, 2, XS // 2 + 1)),
            dma((DATES, 2, XS // 2 + 1)),
            dma((2, ys // 2 + 1)),
            dma((2, ys // 2 + 1)),
            dma((2, ys // 2 + 1)),
            dma((2, ys // 2 + 1)),
            dma((DATES, zs)),
            dma((DATES, zs)),
            dma((scen_n,)),
            dma((scen_n,)),
        ],
        compiler_params=pltpu.CompilerParams(
            collective_id=0, has_side_effects=True, vmem_limit_bytes=48 * 1024 * 1024
        ),
    )(
        shocks,
        loadings,
        vol.reshape(1, width),
        jump_counts,
        jump_noise,
        jump_mean.reshape(1, width),
        jump_vol.reshape(1, width),
        dependencies.T,
        block_slot,
        trade_weights.reshape(2 * trades, BLOCK),
        netting.reshape(1, trades),
    )


def solution(mesh):
    placed = (
        P(None, "scen", None),
        P(None, "fac"),
        P("fac"),
        P(None, "scen", "fac"),
        P(None, "scen", "fac"),
        P("fac"),
        P("fac"),
        P("fac", None),
        P(),
        P("fac", None, None),
        P("fac"),
    )
    return jax.shard_map(
        body,
        mesh=mesh,
        in_specs=placed,
        out_specs=(P(None, "fac", "scen"), P(None, "fac")),
        check_vma=False,
    )
```

```python
import functools

import jax
import jax.numpy as jnp
from jax import lax
from jax.experimental import pallas as pl
from jax.experimental.pallas import tpu as pltpu
from jax.sharding import PartitionSpec as P

BLOCK = 128
SETS = 64
DATES = 2
CORES = 2
XS = 4
P_CUTS = 2
M_CUTS = 2
MESH = pl.DeviceIdType.MESH
F32 = jnp.float32
BF16 = jnp.bfloat16
NT = (((1,), (1,)), ((), ()))
INPUTS = 11
FIRST = (8, 7, 10, 9)
LATER = (0, 1, 3, 4, 2, 5, 6)


class Ring:
    def __init__(self, n, me, axis, device, view, send, recv, cuts):
        self.n, self.me, self.axis, self.device, self.view = n, me, axis, device, view
        self.send, self.recv, self.cuts = send, recv, cuts
        self.last = n // 2

    def pieces(self, way, d):
        half = self.cuts // 2
        if d < self.last:
            return range(self.cuts)
        return range(way * half, (way + 1) * half)

    def owner(self, way, d):
        step = -d if way == 0 else d
        return lax.rem(self.me + step + self.n, self.n)

    def copy(self, way, d, piece, shift):
        ref = self.view(self.owner(way, d - shift), piece)
        to = self.owner(way, -1)
        return pltpu.make_async_remote_copy(
            src_ref=ref,
            dst_ref=ref,
            send_sem=self.send.at[way, d, piece],
            recv_sem=self.recv.at[way, d, piece],
            device_id={self.axis: self.device(to)},
            device_id_type=MESH,
        )

    def begin(self):
        for piece in range(self.cuts):
            for way in range(2):
                if piece in self.pieces(way, 1):
                    self.copy(way, 1, piece, 1).start()

    def step(self, d, also=None):
        for piece in range(self.cuts):
            for way in range(2):
                if piece in self.pieces(way, d):
                    self.copy(way, d, piece, 0).wait_recv()
                    if d < self.last and piece in self.pieces(way, d + 1):
                        self.copy(way, d + 1, piece, 1).start()
                    if also is not None:
                        also(way, d, piece)

    def sent(self):
        for d in range(1, self.last + 1):
            for way in range(2):
                for piece in self.pieces(way, d):
                    self.copy(way, d, piece, 1).wait_send()


def kernel(
    fac_n,
    scen_n,
    *refs,
):
    given, refs = refs[:INPUTS], refs[INPUTS:]
    expo, mean, *refs = refs
    held, refs = refs[:INPUTS], refs[INPUTS:]
    run(fac_n, scen_n, given, held, expo, mean, *refs)


def run(
    fac_n,
    scen_n,
    given,
    held,
    expo,
    mean,
    load_sem,
    w32,
    keys,
    wg,
    marks,
    spread,
    macc,
    mg,
    level,
    pg,
    nets,
    part,
    back,
    sums,
    z_send,
    z_recv,
    x_send,
    x_recv,
    p_send,
    p_recv,
    m_send,
    m_recv,
    c_send,
    c_recv,
    r_send,
    r_recv,
    s_send,
    s_recv,
):
    loads = [
        pltpu.make_async_copy(src, dst, load_sem.at[i])
        for i, (src, dst) in enumerate(zip(given, held))
    ]
    for i in FIRST:
        loads[i].start()
    for i in LATER:
        loads[i].start()
    (shocks, loadings, vol, counts, noise, jump_mean, jump_vol, deps, place, weights, netting) = (
        held
    )
    zs = fac_n // XS
    ys = scen_n // CORES
    rows = shocks.shape[1]
    width = loadings.shape[1]
    local = width // BLOCK
    trades = netting.shape[1]
    jn = BLOCK // scen_n
    fac = lax.axis_index("fac")
    scen = lax.axis_index("scen")
    z, x = fac // XS, lax.rem(fac, XS)
    y, c = scen // CORES, lax.rem(scen, CORES)

    barrier = pltpu.get_barrier_semaphore()
    partners = 0
    for d in range(1, zs):
        pl.semaphore_signal(
            barrier, inc=1, device_id={"fac": lax.rem(z + d, zs) * XS + x}, device_id_type=MESH
        )
        partners += 1
    for d in range(1, XS):
        pl.semaphore_signal(
            barrier, inc=1, device_id={"fac": z * XS + lax.rem(x + d, XS)}, device_id_type=MESH
        )
        partners += 1
    for d in range(1, scen_n):
        pl.semaphore_signal(
            barrier, inc=1, device_id={"scen": lax.rem(scen + d, scen_n)}, device_id_type=MESH
        )
        partners += 1

    for i in FIRST:
        loads[i].wait()

    dep = deps[...]
    slot = jnp.zeros_like(dep)
    for b in range(place.shape[0]):
        slot = jnp.where(dep == b, place[b], slot)
    keys[x, z, :, 0:trades] = slot[0:1]
    keys[x, z, :, trades : 2 * trades] = slot[1:2]
    keys[x, z, :, 2 * trades : 3 * trades] = netting[...]
    w32[...] = weights[...].astype(F32)
    pick = (
        lax.broadcasted_iota(jnp.int32, (jn, BLOCK), 1)
        == lax.broadcasted_iota(jnp.int32, (jn, BLOCK), 0) + scen * jn
    ).astype(F32).astype(BF16)
    chosen = [
        lax.dot_general(
            pick, w32[pl.ds(k, trades, stride=2), :].astype(BF16), NT, preferred_element_type=F32
        )
        for k in range(2)
    ]
    wg[x, z] = jnp.concatenate(chosen, axis=0).astype(BF16)

    def z_copy(kind, d, from_z):
        ref = keys.at[x, from_z] if kind == 0 else wg.at[x, from_z]
        return pltpu.make_async_remote_copy(
            src_ref=ref,
            dst_ref=ref,
            send_sem=z_send.at[kind, d],
            recv_sem=z_recv.at[kind, d],
            device_id={"fac": lax.rem(z + d, zs) * XS + x},
            device_id_type=MESH,
        )

    def x_copy(kind, d, from_x):
        ref = keys.at[from_x] if kind == 0 else wg.at[from_x]
        return pltpu.make_async_remote_copy(
            src_ref=ref,
            dst_ref=ref,
            send_sem=x_send.at[kind, d],
            recv_sem=x_recv.at[kind, d],
            device_id={"fac": z * XS + lax.rem(x + d, XS)},
            device_id_type=MESH,
        )

    pl.semaphore_wait(barrier, partners)
    for kind in range(2):
        for d in range(1, zs):
            z_copy(kind, d, z).start()
    for i in LATER:
        loads[i].wait()

    p_rings = []
    cut_rows = rows // P_CUTS
    for date in range(DATES):

        def p_view(owner, piece, date=date):
            return pg.at[date, owner, pl.ds(piece * cut_rows, cut_rows)]

        p_rings.append(
            Ring(
                zs,
                z,
                "fac",
                lambda i: i * XS + x,
                p_view,
                p_send.at[date],
                p_recv.at[date],
                P_CUTS,
            )
        )

    col_q = lax.broadcasted_iota(jnp.int32, (width, width), 1)
    col_f = (
        lax.rem(lax.div(col_q, jn), local) * BLOCK
        + lax.div(col_q, jn * local) * jn
        + lax.rem(col_q, jn)
    )
    perm = (lax.broadcasted_iota(jnp.int32, (width, width), 0) == col_f).astype(F32).astype(BF16)
    v = vol[...]
    drift = 0.5 * v * v
    for date in range(DATES):
        diffuse = jnp.dot(shocks[date], loadings[...], preferred_element_type=F32)
        number = counts[date].astype(F32)
        change = (
            v * diffuse
            - drift
            + number * jump_mean[...]
            + jnp.sqrt(number) * jump_vol[...] * noise[date].astype(F32)
        )
        now = change if date == 0 else level[...] + change
        if date < DATES - 1:
            level[...] = now
        prices = (jnp.exp(now) - 1.0).astype(BF16)
        pg[date, z] = jnp.dot(prices, perm, preferred_element_type=F32).astype(BF16)

    for kind in range(2):
        for d in range(1, zs):
            z_copy(kind, d, lax.rem(z - d + zs, zs)).wait_recv()
    for kind in range(2):
        for d in (1, XS - 1, 2):
            x_copy(kind, d, x).start()
    for ring in p_rings:
        ring.begin()
    sets = XS * SETS
    macc[...] = jnp.zeros_like(macc)

    def form(owner):
        @pl.loop(0, zs)
        def _(at):
            columns = pl.ds(pl.multiple_of(at * trades, trades), trades)
            key = keys[owner, at]
            line = key[:, 2 * trades : 3 * trades] - sets * z
            marks[:, columns] = jnp.where(
                lax.broadcasted_iota(jnp.int32, (sets, trades), 0) == line, 1.0, 0.0
            ).astype(BF16)
            w = wg[owner, at].astype(F32)
            w0, w1 = w[0:jn], w[jn : 2 * jn]
            first = key[:, 0:trades] - local * x
            second = key[:, trades : 2 * trades] - local * x
            spread[:, columns] = jnp.concatenate(
                [
                    jnp.where(first == b, w0, 0.0) + jnp.where(second == b, w1, 0.0)
                    for b in [
                        to_z * XS * local + of for to_z in range(zs) for of in range(local)
                    ]
                ],
                axis=0,
            ).astype(BF16)

        macc[...] += lax.dot_general(spread[...], marks[...], NT, preferred_element_type=F32)

    form(x)
    for d in (1, XS - 1, 2):
        from_x = lax.rem(x - d + XS, XS)
        for kind in range(2):
            x_copy(kind, d, from_x).wait_recv()
        form(from_x)
    mg[scen] = macc[...].astype(BF16)

    cut_tall = macc.shape[0] // M_CUTS

    def m_view(core):
        def view(owner, piece):
            return mg.at[owner * CORES + core, pl.ds(piece * cut_tall, cut_tall)]

        return view

    m_ring = Ring(ys, y, "scen", lambda i: i * CORES + c, m_view(c), m_send, m_recv, M_CUTS)
    other = 1 - c

    def c_copy(way, d, piece, core):
        ref = m_view(core)(m_ring.owner(way, d), piece)
        return pltpu.make_async_remote_copy(
            src_ref=ref,
            dst_ref=ref,
            send_sem=c_send.at[way, d, piece],
            recv_sem=c_recv.at[way, d, piece],
            device_id={"scen": y * CORES + other},
            device_id_type=MESH,
        )

    def pass_on(way, d, piece):
        c_copy(way, d, piece, c).start()

    c_pieces = [(0, 0, piece) for piece in range(M_CUTS)] + [
        (way, d, piece)
        for d in range(1, ys // 2 + 1)
        for way in range(2)
        for piece in m_ring.pieces(way, d)
    ]
    m_ring.begin()
    for piece in range(M_CUTS):
        pass_on(0, 0, piece)
    for d in range(1, max(ys, zs) // 2 + 1):
        if d <= zs // 2:
            for ring in p_rings:
                ring.step(d)
        if d <= ys // 2:
            m_ring.step(d, pass_on)
    for way, d, piece in c_pieces:
        c_copy(way, d, piece, other).wait_recv()

    def r_copy(date, d, slot_at):
        return pltpu.make_async_remote_copy(
            src_ref=part.at[date, slot_at],
            dst_ref=back.at[date, d],
            send_sem=r_send.at[date, d],
            recv_sem=r_recv.at[date, d],
            device_id={"fac": z * XS + lax.rem(x + d, XS)},
            device_id_type=MESH,
        )

    tall = local * jn
    for date in range(DATES):
        total = None
        for at in range(zs):
            term = jnp.dot(
                pg[date, at],
                mg[:, at * tall : (at + 1) * tall, :].reshape(scen_n * tall, sets),
                preferred_element_type=F32,
            )
            total = term if total is None else total + term
        turned = total.T.reshape(XS, SETS, rows)
        nets[date] = turned
        part[date] = turned.astype(BF16)
        for d in (1, XS - 1, 2):
            r_copy(date, d, lax.rem(x + d, XS)).start()
    for date in range(DATES):
        total = nets[date, x]
        for d in (1, XS - 1, 2):
            r_copy(date, d, 0).wait_recv()
            total = total + back[date, d].astype(F32)
        expo[date] = jnp.maximum(total, 0.0)

    both = jnp.concatenate([expo[date] for date in range(DATES)], axis=0)
    ones = jnp.ones((8, rows), F32)
    row = lax.dot_general(
        ones, both, NT, precision=lax.Precision.HIGHEST, preferred_element_type=F32
    )
    sums[0] = row[0:1]

    def s_copy(d):
        return pltpu.make_async_remote_copy(
            src_ref=sums.at[0],
            dst_ref=sums.at[d],
            send_sem=s_send.at[d],
            recv_sem=s_recv.at[d],
            device_id={"scen": lax.rem(scen + d, scen_n)},
            device_id_type=MESH,
        )

    for d in range(1, scen_n):
        s_copy(d).start()
    for d in range(1, scen_n):
        s_copy(d).wait_recv()
    average = jnp.sum(sums[...], axis=0) / (rows * scen_n)
    for date in range(DATES):
        mean[date : date + 1, :] = average[:, date * SETS : (date + 1) * SETS]

    for kind in range(2):
        for d in range(1, zs):
            z_copy(kind, d, z).wait_send()
        for d in range(1, XS):
            x_copy(kind, d, x).wait_send()
    for ring in p_rings:
        ring.sent()
    m_ring.sent()
    for way, d, piece in c_pieces:
        c_copy(way, d, piece, c).wait_send()
    for date in range(DATES):
        for d in range(1, XS):
            r_copy(date, d, 0).wait_send()
    for d in range(1, scen_n):
        s_copy(d).wait_send()


def body(
    shocks,
    loadings,
    vol,
    jump_counts,
    jump_noise,
    jump_mean,
    jump_vol,
    dependencies,
    block_slot,
    trade_weights,
    netting,
):
    fac_n = lax.axis_size("fac")
    scen_n = lax.axis_size("scen")
    zs = fac_n // XS
    ys = scen_n // CORES
    rows = shocks.shape[1]
    width = loadings.shape[1]
    trades = netting.shape[0]
    local = width // BLOCK
    jn = BLOCK // scen_n
    tall = zs * local * jn
    sets = XS * SETS
    vmem = pl.BlockSpec(memory_space=pltpu.VMEM)
    hbm = pl.BlockSpec(memory_space=pltpu.HBM)
    dma = pltpu.SemaphoreType.DMA
    arrays = (
        shocks,
        loadings,
        vol.reshape(1, width),
        jump_counts,
        jump_noise,
        jump_mean.reshape(1, width),
        jump_vol.reshape(1, width),
        dependencies.T,
        block_slot,
        trade_weights.reshape(2 * trades, BLOCK),
        netting.reshape(1, trades),
    )
    return pl.pallas_call(
        functools.partial(kernel, fac_n, scen_n),
        out_shape=(
            jax.ShapeDtypeStruct((DATES, SETS, rows), F32),
            jax.ShapeDtypeStruct((DATES, SETS), F32),
        ),
        in_specs=[hbm] * INPUTS,
        out_specs=(vmem, vmem),
        scratch_shapes=[
            (pltpu.SMEM if i == 8 else pltpu.VMEM)(a.shape, a.dtype) for i, a in enumerate(arrays)
        ]
        + [
            dma((INPUTS,)),
            pltpu.VMEM((2 * trades, BLOCK), F32),
            pltpu.VMEM((XS, zs, 1, 3 * trades), jnp.int32),
            pltpu.VMEM((XS, zs, 2 * jn, trades), BF16),
            pltpu.VMEM((sets, zs * trades), BF16),
            pltpu.VMEM((tall, zs * trades), BF16),
            pltpu.VMEM((tall, sets), F32),
            pltpu.VMEM((scen_n, tall, sets), BF16),
            pltpu.VMEM((rows, width), F32),
            pltpu.VMEM((DATES, zs, rows, width), BF16),
            pltpu.VMEM((DATES, XS, SETS, rows), F32),
            pltpu.VMEM((DATES, XS, SETS, rows), BF16),
            pltpu.VMEM((DATES, XS, SETS, rows), BF16),
            pltpu.VMEM((scen_n, 1, DATES * SETS), F32),
            dma((2, zs)),
            dma((2, zs)),
            dma((2, XS)),
            dma((2, XS)),
            dma((DATES, 2, zs // 2 + 1, P_CUTS)),
            dma((DATES, 2, zs // 2 + 1, P_CUTS)),
            dma((2, ys // 2 + 1, M_CUTS)),
            dma((2, ys // 2 + 1, M_CUTS)),
            dma((2, ys // 2 + 1, M_CUTS)),
            dma((2, ys // 2 + 1, M_CUTS)),
            dma((DATES, XS)),
            dma((DATES, XS)),
            dma((scen_n,)),
            dma((scen_n,)),
        ],
        compiler_params=pltpu.CompilerParams(
            collective_id=0, has_side_effects=True, vmem_limit_bytes=60 * 1024 * 1024
        ),
    )(*arrays)


def solution(mesh):
    placed = (
        P(None, "scen", None),
        P(None, "fac"),
        P("fac"),
        P(None, "scen", "fac"),
        P(None, "scen", "fac"),
        P("fac"),
        P("fac"),
        P("fac", None),
        P(),
        P("fac", None, None),
        P("fac"),
    )
    return jax.shard_map(
        body,
        mesh=mesh,
        in_specs=placed,
        out_specs=(P(None, "fac", "scen"), P(None, "fac")),
        check_vma=False,
    )
```

```python
import functools

import jax
import jax.numpy as jnp
from jax import lax
from jax.experimental import pallas as pl
from jax.experimental.pallas import tpu as pltpu
from jax.sharding import PartitionSpec as P

BLOCK = 128
SETS = 64
DATES = 2
CORES = 2
XS = 4
P_CUTS = 2
M_CUTS = 2
MESH = pl.DeviceIdType.MESH
F32 = jnp.float32
BF16 = jnp.bfloat16
NT = (((1,), (1,)), ((), ()))
INPUTS = 11
FIRST = (8, 7, 10, 9)
LATER = (0, 1, 3, 4, 2, 5, 6)


class Ring:
    def __init__(self, n, me, axis, device, view, send, recv, cuts, hops):
        self.n, self.me, self.axis, self.device, self.view = n, me, axis, device, view
        self.send, self.recv, self.cuts, self.hops = send, recv, cuts, hops
        self.last = n // 2

    def pieces(self, way, d):
        half = self.cuts // 2
        if d < self.last:
            return range(self.cuts)
        return range(way * half, (way + 1) * half)

    def owner(self, way, d):
        step = -d if way == 0 else d
        return lax.rem(self.me + step + self.n, self.n)

    def copy(self, way, d, piece, shift):
        ref = self.view(self.owner(way, d - shift), piece)
        to = self.owner(way, -self.hops[d])
        return pltpu.make_async_remote_copy(
            src_ref=ref,
            dst_ref=ref,
            send_sem=self.send.at[way, d, piece],
            recv_sem=self.recv.at[way, d, piece],
            device_id={self.axis: self.device(to)},
            device_id_type=MESH,
        )

    def start(self, way, d, piece):
        self.copy(way, d, piece, self.hops[d]).start()

    def begin(self):
        for d in range(self.last, 0, -1):
            for piece in range(self.cuts):
                for way in range(2):
                    if d == self.hops[d] and piece in self.pieces(way, d):
                        self.start(way, d, piece)

    def step(self, d, also=None):
        if d > self.last:
            return
        for piece in range(self.cuts):
            for way in range(2):
                if piece in self.pieces(way, d):
                    self.copy(way, d, piece, 0).wait_recv()
                    for later in range(d + 1, self.last + 1):
                        if later - self.hops[later] == d and piece in self.pieces(way, later):
                            self.start(way, later, piece)
                    if also is not None:
                        also(way, d, piece)

    def sent(self):
        for d in range(1, self.last + 1):
            for way in range(2):
                for piece in self.pieces(way, d):
                    self.copy(way, d, piece, self.hops[d]).wait_send()


def kernel(
    fac_n,
    scen_n,
    *refs,
):
    given, refs = refs[:INPUTS], refs[INPUTS:]
    expo, mean, *refs = refs
    held, refs = refs[:INPUTS], refs[INPUTS:]
    run(fac_n, scen_n, given, held, expo, mean, *refs)


def run(
    fac_n,
    scen_n,
    given,
    held,
    expo,
    mean,
    load_sem,
    w32,
    keys,
    wg,
    marks,
    spread,
    macc,
    mg,
    level,
    pg,
    nets,
    part,
    back,
    sums,
    z_send,
    z_recv,
    x_send,
    x_recv,
    p_send,
    p_recv,
    m_send,
    m_recv,
    c_send,
    c_recv,
    r_send,
    r_recv,
    s_send,
    s_recv,
):
    loads = [
        pltpu.make_async_copy(src, dst, load_sem.at[i])
        for i, (src, dst) in enumerate(zip(given, held))
    ]
    for i in FIRST:
        loads[i].start()
    for i in LATER:
        loads[i].start()
    (shocks, loadings, vol, counts, noise, jump_mean, jump_vol, deps, place, weights, netting) = (
        held
    )
    zs = fac_n // XS
    ys = scen_n // CORES
    rows = shocks.shape[1]
    width = loadings.shape[1]
    local = width // BLOCK
    trades = netting.shape[1]
    jn = BLOCK // scen_n
    fac = lax.axis_index("fac")
    scen = lax.axis_index("scen")
    z, x = fac // XS, lax.rem(fac, XS)
    y, c = scen // CORES, lax.rem(scen, CORES)

    barrier = pltpu.get_barrier_semaphore()
    partners = 0
    for d in range(1, zs):
        pl.semaphore_signal(
            barrier, inc=1, device_id={"fac": lax.rem(z + d, zs) * XS + x}, device_id_type=MESH
        )
        partners += 1
    for d in range(1, XS):
        pl.semaphore_signal(
            barrier, inc=1, device_id={"fac": z * XS + lax.rem(x + d, XS)}, device_id_type=MESH
        )
        partners += 1
    for d in range(1, scen_n):
        pl.semaphore_signal(
            barrier, inc=1, device_id={"scen": lax.rem(scen + d, scen_n)}, device_id_type=MESH
        )
        partners += 1

    for i in FIRST:
        loads[i].wait()

    dep = deps[...]
    slot = jnp.zeros_like(dep)
    for b in range(place.shape[0]):
        slot = jnp.where(dep == b, place[b], slot)
    keys[x, 0, :, 0:trades] = slot[0:1]
    keys[x, 0, :, trades : 2 * trades] = slot[1:2]
    keys[x, 0, :, 2 * trades : 3 * trades] = netting[...]
    w32[...] = weights[...].astype(F32)
    pick = (
        lax.broadcasted_iota(jnp.int32, (jn, BLOCK), 1)
        == lax.broadcasted_iota(jnp.int32, (jn, BLOCK), 0) + scen * jn
    ).astype(F32).astype(BF16)
    chosen = [
        lax.dot_general(
            pick, w32[pl.ds(k, trades, stride=2), :].astype(BF16), NT, preferred_element_type=F32
        )
        for k in range(2)
    ]
    wg[x, 0] = jnp.concatenate(chosen, axis=0).astype(BF16)

    near = [0]
    for d in range(1, zs // 2 + 1):
        near += [d] if 2 * d == zs else [d, zs - d]
    cut = zs * 5 // 8
    groups = ((0, cut), (cut, zs))

    def z_copy(kind, d):
        buffer = keys if kind == 0 else wg
        return pltpu.make_async_remote_copy(
            src_ref=buffer.at[x, 0],
            dst_ref=buffer.at[x, near.index(d)],
            send_sem=z_send.at[kind, d],
            recv_sem=z_recv.at[kind, d],
            device_id={"fac": lax.rem(z + d, zs) * XS + x},
            device_id_type=MESH,
        )

    def x_copy(kind, d, piece, from_x):
        buffer = keys if kind == 0 else wg
        low, high = groups[piece]
        ref = buffer.at[from_x, pl.ds(low, high - low)]
        return pltpu.make_async_remote_copy(
            src_ref=ref,
            dst_ref=ref,
            send_sem=x_send.at[kind, d, piece],
            recv_sem=x_recv.at[kind, d, piece],
            device_id={"fac": z * XS + lax.rem(x + d, XS)},
            device_id_type=MESH,
        )

    pl.semaphore_wait(barrier, partners)
    for d in near[:0:-1]:
        for kind in range(2):
            z_copy(kind, d).start()
    for i in LATER:
        loads[i].wait()

    p_rings = []
    cut_rows = rows // P_CUTS
    for date in range(DATES):

        def p_view(owner, piece, date=date):
            return pg.at[date, owner, pl.ds(piece * cut_rows, cut_rows)]

        p_rings.append(
            Ring(
                zs,
                z,
                "fac",
                lambda i: i * XS + x,
                p_view,
                p_send.at[date],
                p_recv.at[date],
                P_CUTS,
                (0, 1, 1, 1, 1),
            )
        )

    col_q = lax.broadcasted_iota(jnp.int32, (width, width), 1)
    col_f = (
        lax.rem(lax.div(col_q, jn), local) * BLOCK
        + lax.div(col_q, jn * local) * jn
        + lax.rem(col_q, jn)
    )
    perm = (lax.broadcasted_iota(jnp.int32, (width, width), 0) == col_f).astype(F32).astype(BF16)
    v = vol[...]
    drift = 0.5 * v * v
    for date in range(DATES):
        diffuse = jnp.dot(shocks[date], loadings[...], preferred_element_type=F32)
        number = counts[date].astype(F32)
        change = (
            v * diffuse
            - drift
            + number * jump_mean[...]
            + jnp.sqrt(number) * jump_vol[...] * noise[date].astype(F32)
        )
        now = change if date == 0 else level[...] + change
        if date < DATES - 1:
            level[...] = now
        prices = (jnp.exp(now) - 1.0).astype(BF16)
        pg[date, z] = jnp.dot(prices, perm, preferred_element_type=F32).astype(BF16)
        p_rings[date].begin()

    for piece, (low, high) in enumerate(groups):
        for d in near[max(low, 1) : high]:
            for kind in range(2):
                z_copy(kind, d).wait_recv()
        for d in (2, 1, XS - 1):
            for kind in range(2):
                x_copy(kind, d, piece, x).start()

    sets = XS * SETS
    macc[...] = jnp.zeros_like(macc)

    def form(owner):
        @pl.loop(0, zs)
        def _(at):
            columns = pl.ds(pl.multiple_of(at * trades, trades), trades)
            key = keys[owner, at]
            line = key[:, 2 * trades : 3 * trades] - sets * z
            marks[:, columns] = jnp.where(
                lax.broadcasted_iota(jnp.int32, (sets, trades), 0) == line, 1.0, 0.0
            ).astype(BF16)
            w = wg[owner, at].astype(F32)
            w0, w1 = w[0:jn], w[jn : 2 * jn]
            first = key[:, 0:trades] - local * x
            second = key[:, trades : 2 * trades] - local * x
            spread[:, columns] = jnp.concatenate(
                [
                    jnp.where(first == b, w0, 0.0) + jnp.where(second == b, w1, 0.0)
                    for b in [
                        to_z * XS * local + of for to_z in range(zs) for of in range(local)
                    ]
                ],
                axis=0,
            ).astype(BF16)

        macc[...] += lax.dot_general(spread[...], marks[...], NT, preferred_element_type=F32)

    def form_from(d):
        from_x = lax.rem(x - d + XS, XS)
        for piece in range(2):
            for kind in range(2):
                x_copy(kind, d, piece, from_x).wait_recv()
        form(from_x)

    form(x)
    for ring in p_rings:
        ring.step(1)
    form_from(1)
    form_from(XS - 1)
    p_rings[0].step(2)
    form_from(2)
    mg[scen] = macc[...].astype(BF16)

    cut_tall = macc.shape[0] // M_CUTS

    def m_view(core):
        def view(owner, piece):
            return mg.at[owner * CORES + core, pl.ds(piece * cut_tall, cut_tall)]

        return view

    m_ring = Ring(
        ys,
        y,
        "scen",
        lambda i: i * CORES + c,
        m_view(c),
        m_send,
        m_recv,
        M_CUTS,
        (0, 1, 2, 1, 2),
    )
    other = 1 - c

    def c_copy(way, d, piece, core):
        ref = m_view(core)(m_ring.owner(way, d), piece)
        return pltpu.make_async_remote_copy(
            src_ref=ref,
            dst_ref=ref,
            send_sem=c_send.at[way, d, piece],
            recv_sem=c_recv.at[way, d, piece],
            device_id={"scen": y * CORES + other},
            device_id_type=MESH,
        )

    def pass_on(way, d, piece):
        c_copy(way, d, piece, c).start()

    c_pieces = [(0, 0, piece) for piece in range(M_CUTS)] + [
        (way, d, piece)
        for d in range(1, ys // 2 + 1)
        for way in range(2)
        for piece in m_ring.pieces(way, d)
    ]
    m_ring.begin()
    for piece in range(M_CUTS):
        pass_on(0, 0, piece)
    p_rings[1].step(2)
    p_rings[0].step(3)
    m_ring.step(2, pass_on)
    m_ring.step(1, pass_on)
    p_rings[1].step(3)
    m_ring.step(3, pass_on)
    m_ring.step(4, pass_on)
    for ring in p_rings:
        ring.step(4)
    for way, d, piece in c_pieces:
        c_copy(way, d, piece, other).wait_recv()

    def r_copy(date, d, slot_at):
        return pltpu.make_async_remote_copy(
            src_ref=part.at[date, slot_at],
            dst_ref=back.at[date, d],
            send_sem=r_send.at[date, d],
            recv_sem=r_recv.at[date, d],
            device_id={"fac": z * XS + lax.rem(x + d, XS)},
            device_id_type=MESH,
        )

    tall = local * jn
    for date in range(DATES):
        total = None
        for at in range(zs):
            term = jnp.dot(
                pg[date, at],
                mg[:, at * tall : (at + 1) * tall, :].reshape(scen_n * tall, sets),
                preferred_element_type=F32,
            )
            total = term if total is None else total + term
        turned = total.T.reshape(XS, SETS, rows)
        nets[date] = turned
        part[date] = turned.astype(BF16)
        for d in (1, XS - 1, 2):
            r_copy(date, d, lax.rem(x + d, XS)).start()
    for date in range(DATES):
        total = nets[date, x]
        for d in (1, XS - 1, 2):
            r_copy(date, d, 0).wait_recv()
            total = total + back[date, d].astype(F32)
        expo[date] = jnp.maximum(total, 0.0)

    both = jnp.concatenate([expo[date] for date in range(DATES)], axis=0)
    ones = jnp.ones((8, rows), F32)
    row = lax.dot_general(
        ones, both, NT, precision=lax.Precision.HIGHEST, preferred_element_type=F32
    )
    sums[0] = row[0:1]

    def s_copy(d):
        return pltpu.make_async_remote_copy(
            src_ref=sums.at[0],
            dst_ref=sums.at[d],
            send_sem=s_send.at[d],
            recv_sem=s_recv.at[d],
            device_id={"scen": lax.rem(scen + d, scen_n)},
            device_id_type=MESH,
        )

    for d in range(1, scen_n):
        s_copy(d).start()
    for d in range(1, scen_n):
        s_copy(d).wait_recv()
    average = jnp.sum(sums[...], axis=0) / (rows * scen_n)
    for date in range(DATES):
        mean[date : date + 1, :] = average[:, date * SETS : (date + 1) * SETS]

    for kind in range(2):
        for d in range(1, zs):
            z_copy(kind, d).wait_send()
        for d in range(1, XS):
            for piece in range(2):
                x_copy(kind, d, piece, x).wait_send()
    for ring in p_rings:
        ring.sent()
    m_ring.sent()
    for way, d, piece in c_pieces:
        c_copy(way, d, piece, c).wait_send()
    for date in range(DATES):
        for d in range(1, XS):
            r_copy(date, d, 0).wait_send()
    for d in range(1, scen_n):
        s_copy(d).wait_send()


def body(
    shocks,
    loadings,
    vol,
    jump_counts,
    jump_noise,
    jump_mean,
    jump_vol,
    dependencies,
    block_slot,
    trade_weights,
    netting,
):
    fac_n = lax.axis_size("fac")
    scen_n = lax.axis_size("scen")
    zs = fac_n // XS
    ys = scen_n // CORES
    rows = shocks.shape[1]
    width = loadings.shape[1]
    trades = netting.shape[0]
    local = width // BLOCK
    jn = BLOCK // scen_n
    tall = zs * local * jn
    sets = XS * SETS
    vmem = pl.BlockSpec(memory_space=pltpu.VMEM)
    hbm = pl.BlockSpec(memory_space=pltpu.HBM)
    dma = pltpu.SemaphoreType.DMA
    arrays = (
        shocks,
        loadings,
        vol.reshape(1, width),
        jump_counts,
        jump_noise,
        jump_mean.reshape(1, width),
        jump_vol.reshape(1, width),
        dependencies.T,
        block_slot,
        trade_weights.reshape(2 * trades, BLOCK),
        netting.reshape(1, trades),
    )
    return pl.pallas_call(
        functools.partial(kernel, fac_n, scen_n),
        out_shape=(
            jax.ShapeDtypeStruct((DATES, SETS, rows), F32),
            jax.ShapeDtypeStruct((DATES, SETS), F32),
        ),
        in_specs=[hbm] * INPUTS,
        out_specs=(vmem, vmem),
        scratch_shapes=[
            (pltpu.SMEM if i == 8 else pltpu.VMEM)(a.shape, a.dtype) for i, a in enumerate(arrays)
        ]
        + [
            dma((INPUTS,)),
            pltpu.VMEM((2 * trades, BLOCK), F32),
            pltpu.VMEM((XS, zs, 1, 3 * trades), jnp.int32),
            pltpu.VMEM((XS, zs, 2 * jn, trades), BF16),
            pltpu.VMEM((sets, zs * trades), BF16),
            pltpu.VMEM((tall, zs * trades), BF16),
            pltpu.VMEM((tall, sets), F32),
            pltpu.VMEM((scen_n, tall, sets), BF16),
            pltpu.VMEM((rows, width), F32),
            pltpu.VMEM((DATES, zs, rows, width), BF16),
            pltpu.VMEM((DATES, XS, SETS, rows), F32),
            pltpu.VMEM((DATES, XS, SETS, rows), BF16),
            pltpu.VMEM((DATES, XS, SETS, rows), BF16),
            pltpu.VMEM((scen_n, 1, DATES * SETS), F32),
            dma((2, zs)),
            dma((2, zs)),
            dma((2, XS, 2)),
            dma((2, XS, 2)),
            dma((DATES, 2, zs // 2 + 1, P_CUTS)),
            dma((DATES, 2, zs // 2 + 1, P_CUTS)),
            dma((2, ys // 2 + 1, M_CUTS)),
            dma((2, ys // 2 + 1, M_CUTS)),
            dma((2, ys // 2 + 1, M_CUTS)),
            dma((2, ys // 2 + 1, M_CUTS)),
            dma((DATES, XS)),
            dma((DATES, XS)),
            dma((scen_n,)),
            dma((scen_n,)),
        ],
        compiler_params=pltpu.CompilerParams(
            collective_id=0, has_side_effects=True, vmem_limit_bytes=60 * 1024 * 1024
        ),
    )(*arrays)


def solution(mesh):
    placed = (
        P(None, "scen", None),
        P(None, "fac"),
        P("fac"),
        P(None, "scen", "fac"),
        P(None, "scen", "fac"),
        P("fac"),
        P("fac"),
        P("fac", None),
        P(),
        P("fac", None, None),
        P("fac"),
    )
    return jax.shard_map(
        body,
        mesh=mesh,
        in_specs=placed,
        out_specs=(P(None, "fac", "scen"), P(None, "fac")),
        check_vma=False,
    )
```

```python
import functools

import jax
import jax.numpy as jnp
from jax import lax
from jax.experimental import pallas as pl
from jax.experimental.pallas import tpu as pltpu
from jax.sharding import PartitionSpec as P

BLOCK = 128
SETS = 64
DATES = 2
CORES = 2
XS = 4
P_CUTS = 2
M_CUTS = 2
MESH = pl.DeviceIdType.MESH
F32 = jnp.float32
BF16 = jnp.bfloat16
NT = (((1,), (1,)), ((), ()))
INPUTS = 11
FIRST = (8, 7, 10, 9)
LATER = (0, 1, 3, 4, 2, 5, 6)


class Ring:
    def __init__(self, n, me, axis, device, view, send, recv, cuts, hops):
        self.n, self.me, self.axis, self.device, self.view = n, me, axis, device, view
        self.send, self.recv, self.cuts, self.hops = send, recv, cuts, hops
        self.last = n // 2

    def pieces(self, way, d):
        half = self.cuts // 2
        if d < self.last:
            return range(self.cuts)
        return range(way * half, (way + 1) * half)

    def owner(self, way, d):
        step = -d if way == 0 else d
        return lax.rem(self.me + step + self.n, self.n)

    def copy(self, way, d, piece, shift):
        ref = self.view(self.owner(way, d - shift), piece)
        to = self.owner(way, -self.hops[d])
        return pltpu.make_async_remote_copy(
            src_ref=ref,
            dst_ref=ref,
            send_sem=self.send.at[way, d, piece],
            recv_sem=self.recv.at[way, d, piece],
            device_id={self.axis: self.device(to)},
            device_id_type=MESH,
        )

    def start(self, way, d, piece):
        self.copy(way, d, piece, self.hops[d]).start()

    def begin(self):
        for d in range(self.last, 0, -1):
            for piece in range(self.cuts):
                for way in range(2):
                    if d == self.hops[d] and piece in self.pieces(way, d):
                        self.start(way, d, piece)

    def step(self, d, also=None):
        if d > self.last:
            return
        for piece in range(self.cuts):
            for way in range(2):
                if piece in self.pieces(way, d):
                    self.copy(way, d, piece, 0).wait_recv()
                    for later in range(d + 1, self.last + 1):
                        if later - self.hops[later] == d and piece in self.pieces(way, later):
                            self.start(way, later, piece)
                    if also is not None:
                        also(way, d, piece)

    def sent(self):
        for d in range(1, self.last + 1):
            for way in range(2):
                for piece in self.pieces(way, d):
                    self.copy(way, d, piece, self.hops[d]).wait_send()


def kernel(
    fac_n,
    scen_n,
    *refs,
):
    given, refs = refs[:INPUTS], refs[INPUTS:]
    expo, mean, *refs = refs
    held, refs = refs[:INPUTS], refs[INPUTS:]
    run(fac_n, scen_n, given, held, expo, mean, *refs)


def run(
    fac_n,
    scen_n,
    given,
    held,
    expo,
    mean,
    load_sem,
    w32,
    keys,
    wg,
    marks,
    spread,
    macc,
    mg,
    level,
    pg,
    nets,
    part,
    back,
    sums,
    z_send,
    z_recv,
    x_send,
    x_recv,
    p_send,
    p_recv,
    m_send,
    m_recv,
    c_send,
    c_recv,
    r_send,
    r_recv,
    s_send,
    s_recv,
):
    loads = [
        pltpu.make_async_copy(src, dst, load_sem.at[i])
        for i, (src, dst) in enumerate(zip(given, held))
    ]
    for i in FIRST:
        loads[i].start()
    for i in LATER:
        loads[i].start()
    (shocks, loadings, vol, counts, noise, jump_mean, jump_vol, deps, place, weights, netting) = (
        held
    )
    zs = fac_n // XS
    ys = scen_n // CORES
    rows = shocks.shape[1]
    width = loadings.shape[1]
    local = width // BLOCK
    trades = netting.shape[1]
    jn = BLOCK // scen_n
    fac = lax.axis_index("fac")
    scen = lax.axis_index("scen")
    z, x = fac // XS, lax.rem(fac, XS)
    y, c = scen // CORES, lax.rem(scen, CORES)

    barrier = pltpu.get_barrier_semaphore()
    partners = 0
    for d in range(1, zs):
        pl.semaphore_signal(
            barrier, inc=1, device_id={"fac": lax.rem(z + d, zs) * XS + x}, device_id_type=MESH
        )
        partners += 1
    for d in range(1, XS):
        pl.semaphore_signal(
            barrier, inc=1, device_id={"fac": z * XS + lax.rem(x + d, XS)}, device_id_type=MESH
        )
        partners += 1
    for d in range(1, scen_n):
        pl.semaphore_signal(
            barrier, inc=1, device_id={"scen": lax.rem(scen + d, scen_n)}, device_id_type=MESH
        )
        partners += 1

    for i in FIRST:
        loads[i].wait()

    dep = deps[...]
    slot = jnp.zeros_like(dep)
    for b in range(place.shape[0]):
        slot = jnp.where(dep == b, place[b], slot)
    keys[x, 0, :, 0:trades] = slot[0:1]
    keys[x, 0, :, trades : 2 * trades] = slot[1:2]
    keys[x, 0, :, 2 * trades : 3 * trades] = netting[...]
    w32[...] = weights[...].astype(F32)
    pick = (
        lax.broadcasted_iota(jnp.int32, (jn, BLOCK), 1)
        == lax.broadcasted_iota(jnp.int32, (jn, BLOCK), 0) + scen * jn
    ).astype(F32).astype(BF16)
    chosen = [
        lax.dot_general(
            pick, w32[pl.ds(k, trades, stride=2), :].astype(BF16), NT, preferred_element_type=F32
        )
        for k in range(2)
    ]
    wg[x, 0] = jnp.concatenate(chosen, axis=0).astype(BF16)

    near = [0]
    for d in range(1, zs // 2 + 1):
        near += [d] if 2 * d == zs else [d, zs - d]
    cut = zs * 5 // 8
    groups = ((0, cut), (cut, zs))

    def z_copy(kind, d):
        buffer = keys if kind == 0 else wg
        return pltpu.make_async_remote_copy(
            src_ref=buffer.at[x, 0],
            dst_ref=buffer.at[x, near.index(d)],
            send_sem=z_send.at[kind, d],
            recv_sem=z_recv.at[kind, d],
            device_id={"fac": lax.rem(z + d, zs) * XS + x},
            device_id_type=MESH,
        )

    def x_copy(kind, d, piece, from_x):
        buffer = keys if kind == 0 else wg
        low, high = groups[piece]
        ref = buffer.at[from_x, pl.ds(low, high - low)]
        return pltpu.make_async_remote_copy(
            src_ref=ref,
            dst_ref=ref,
            send_sem=x_send.at[kind, d, piece],
            recv_sem=x_recv.at[kind, d, piece],
            device_id={"fac": z * XS + lax.rem(x + d, XS)},
            device_id_type=MESH,
        )

    pl.semaphore_wait(barrier, partners)
    for d in near[:0:-1]:
        for kind in range(2):
            z_copy(kind, d).start()
    for i in LATER:
        loads[i].wait()

    p_rings = []
    cut_rows = rows // P_CUTS
    for date in range(DATES):

        def p_view(owner, piece, date=date):
            return pg.at[date, owner, pl.ds(piece * cut_rows, cut_rows)]

        p_rings.append(
            Ring(
                zs,
                z,
                "fac",
                lambda i: i * XS + x,
                p_view,
                p_send.at[date],
                p_recv.at[date],
                P_CUTS,
                (0, 1, 1, 1, 1),
            )
        )

    col_q = lax.broadcasted_iota(jnp.int32, (width, width), 1)
    col_f = (
        lax.rem(lax.div(col_q, jn), local) * BLOCK
        + lax.div(col_q, jn * local) * jn
        + lax.rem(col_q, jn)
    )
    perm = (lax.broadcasted_iota(jnp.int32, (width, width), 0) == col_f).astype(F32).astype(BF16)
    v = vol[...]
    drift = 0.5 * v * v
    for date in range(DATES):
        diffuse = jnp.dot(shocks[date], loadings[...], preferred_element_type=F32)
        number = counts[date].astype(F32)
        change = (
            v * diffuse
            - drift
            + number * jump_mean[...]
            + jnp.sqrt(number) * jump_vol[...] * noise[date].astype(F32)
        )
        now = change if date == 0 else level[...] + change
        if date < DATES - 1:
            level[...] = now
        prices = (jnp.exp(now) - 1.0).astype(BF16)
        pg[date, z] = jnp.dot(prices, perm, preferred_element_type=F32).astype(BF16)
        p_rings[date].begin()

    sets = XS * SETS
    macc[...] = jnp.zeros_like(macc)

    def form(owner, piece):
        low, high = groups[piece]

        @pl.loop(low, high)
        def _(at):
            columns = pl.ds(pl.multiple_of(at * trades, trades), trades)
            key = keys[owner, at]
            line = key[:, 2 * trades : 3 * trades] - sets * z
            marks[:, columns] = jnp.where(
                lax.broadcasted_iota(jnp.int32, (sets, trades), 0) == line, 1.0, 0.0
            ).astype(BF16)
            w = wg[owner, at].astype(F32)
            w0, w1 = w[0:jn], w[jn : 2 * jn]
            first = key[:, 0:trades] - local * x
            second = key[:, trades : 2 * trades] - local * x
            spread[:, columns] = jnp.concatenate(
                [
                    jnp.where(first == b, w0, 0.0) + jnp.where(second == b, w1, 0.0)
                    for b in [
                        to_z * XS * local + of for to_z in range(zs) for of in range(local)
                    ]
                ],
                axis=0,
            ).astype(BF16)

        columns = pl.ds(low * trades, (high - low) * trades)
        macc[...] += lax.dot_general(
            spread[:, columns], marks[:, columns], NT, preferred_element_type=F32
        )

    def form_from(d, piece):
        from_x = lax.rem(x - d + XS, XS)
        for kind in range(2):
            x_copy(kind, d, piece, from_x).wait_recv()
        form(from_x, piece)

    for piece, (low, high) in enumerate(groups):
        for d in near[max(low, 1) : high]:
            for kind in range(2):
                z_copy(kind, d).wait_recv()
        for d in (2, 1, XS - 1):
            for kind in range(2):
                x_copy(kind, d, piece, x).start()
        if piece == 1:
            p_rings[0].step(1)
        form(x, piece)
    form_from(1, 0)
    form_from(XS - 1, 0)
    form_from(2, 0)
    p_rings[1].step(1)
    form_from(1, 1)
    form_from(XS - 1, 1)
    form_from(2, 1)
    mg[scen] = macc[...].astype(BF16)

    cut_tall = macc.shape[0] // M_CUTS

    def m_view(core):
        def view(owner, piece):
            return mg.at[owner * CORES + core, pl.ds(piece * cut_tall, cut_tall)]

        return view

    m_ring = Ring(
        ys,
        y,
        "scen",
        lambda i: i * CORES + c,
        m_view(c),
        m_send,
        m_recv,
        M_CUTS,
        (0, 1, 2, 1, 2),
    )
    other = 1 - c

    def c_copy(way, d, piece, core):
        ref = m_view(core)(m_ring.owner(way, d), piece)
        return pltpu.make_async_remote_copy(
            src_ref=ref,
            dst_ref=ref,
            send_sem=c_send.at[way, d, piece],
            recv_sem=c_recv.at[way, d, piece],
            device_id={"scen": y * CORES + other},
            device_id_type=MESH,
        )

    def pass_on(way, d, piece):
        c_copy(way, d, piece, c).start()

    c_pieces = [(0, 0, piece) for piece in range(M_CUTS)] + [
        (way, d, piece)
        for d in range(1, ys // 2 + 1)
        for way in range(2)
        for piece in m_ring.pieces(way, d)
    ]
    m_ring.begin()
    for piece in range(M_CUTS):
        pass_on(0, 0, piece)
    p_rings[0].step(2)
    p_rings[1].step(2)
    m_ring.step(2, pass_on)
    p_rings[0].step(3)
    m_ring.step(1, pass_on)
    p_rings[1].step(3)
    m_ring.step(3, pass_on)
    m_ring.step(4, pass_on)
    for ring in p_rings:
        ring.step(4)
    for way, d, piece in c_pieces:
        c_copy(way, d, piece, other).wait_recv()

    def r_copy(date, d, slot_at):
        return pltpu.make_async_remote_copy(
            src_ref=part.at[date, slot_at],
            dst_ref=back.at[date, d],
            send_sem=r_send.at[date, d],
            recv_sem=r_recv.at[date, d],
            device_id={"fac": z * XS + lax.rem(x + d, XS)},
            device_id_type=MESH,
        )

    tall = local * jn
    for date in range(DATES):
        total = None
        for at in range(zs):
            term = jnp.dot(
                pg[date, at],
                mg[:, at * tall : (at + 1) * tall, :].reshape(scen_n * tall, sets),
                preferred_element_type=F32,
            )
            total = term if total is None else total + term
        turned = total.T.reshape(XS, SETS, rows)
        nets[date] = turned
        part[date] = turned.astype(BF16)
        for d in (1, XS - 1, 2):
            r_copy(date, d, lax.rem(x + d, XS)).start()
    for date in range(DATES):
        total = nets[date, x]
        for d in (1, XS - 1, 2):
            r_copy(date, d, 0).wait_recv()
            total = total + back[date, d].astype(F32)
        expo[date] = jnp.maximum(total, 0.0)

    both = jnp.concatenate([expo[date] for date in range(DATES)], axis=0)
    high = both.astype(BF16)
    low = (both - high.astype(F32)).astype(BF16)
    row = lax.dot_general(
        jnp.ones((8, 2 * rows), BF16),
        jnp.concatenate([high, low], axis=1),
        NT,
        preferred_element_type=F32,
    )
    sums[0] = row[0:1]

    def s_copy(d):
        return pltpu.make_async_remote_copy(
            src_ref=sums.at[0],
            dst_ref=sums.at[d],
            send_sem=s_send.at[d],
            recv_sem=s_recv.at[d],
            device_id={"scen": lax.rem(scen + d, scen_n)},
            device_id_type=MESH,
        )

    for d in range(1, scen_n):
        s_copy(d).start()
    for d in range(1, scen_n):
        s_copy(d).wait_recv()
    average = jnp.sum(sums[...], axis=0) / (rows * scen_n)
    for date in range(DATES):
        mean[date : date + 1, :] = average[:, date * SETS : (date + 1) * SETS]

    for kind in range(2):
        for d in range(1, zs):
            z_copy(kind, d).wait_send()
        for d in range(1, XS):
            for piece in range(2):
                x_copy(kind, d, piece, x).wait_send()
    for ring in p_rings:
        ring.sent()
    m_ring.sent()
    for way, d, piece in c_pieces:
        c_copy(way, d, piece, c).wait_send()
    for date in range(DATES):
        for d in range(1, XS):
            r_copy(date, d, 0).wait_send()
    for d in range(1, scen_n):
        s_copy(d).wait_send()


def body(
    shocks,
    loadings,
    vol,
    jump_counts,
    jump_noise,
    jump_mean,
    jump_vol,
    dependencies,
    block_slot,
    trade_weights,
    netting,
):
    fac_n = lax.axis_size("fac")
    scen_n = lax.axis_size("scen")
    zs = fac_n // XS
    ys = scen_n // CORES
    rows = shocks.shape[1]
    width = loadings.shape[1]
    trades = netting.shape[0]
    local = width // BLOCK
    jn = BLOCK // scen_n
    tall = zs * local * jn
    sets = XS * SETS
    vmem = pl.BlockSpec(memory_space=pltpu.VMEM)
    hbm = pl.BlockSpec(memory_space=pltpu.HBM)
    dma = pltpu.SemaphoreType.DMA
    arrays = (
        shocks,
        loadings,
        vol.reshape(1, width),
        jump_counts,
        jump_noise,
        jump_mean.reshape(1, width),
        jump_vol.reshape(1, width),
        dependencies.T,
        block_slot,
        trade_weights.reshape(2 * trades, BLOCK),
        netting.reshape(1, trades),
    )
    return pl.pallas_call(
        functools.partial(kernel, fac_n, scen_n),
        out_shape=(
            jax.ShapeDtypeStruct((DATES, SETS, rows), F32),
            jax.ShapeDtypeStruct((DATES, SETS), F32),
        ),
        in_specs=[hbm] * INPUTS,
        out_specs=(vmem, vmem),
        scratch_shapes=[
            (pltpu.SMEM if i == 8 else pltpu.VMEM)(a.shape, a.dtype) for i, a in enumerate(arrays)
        ]
        + [
            dma((INPUTS,)),
            pltpu.VMEM((2 * trades, BLOCK), F32),
            pltpu.VMEM((XS, zs, 1, 3 * trades), jnp.int32),
            pltpu.VMEM((XS, zs, 2 * jn, trades), BF16),
            pltpu.VMEM((sets, zs * trades), BF16),
            pltpu.VMEM((tall, zs * trades), BF16),
            pltpu.VMEM((tall, sets), F32),
            pltpu.VMEM((scen_n, tall, sets), BF16),
            pltpu.VMEM((rows, width), F32),
            pltpu.VMEM((DATES, zs, rows, width), BF16),
            pltpu.VMEM((DATES, XS, SETS, rows), F32),
            pltpu.VMEM((DATES, XS, SETS, rows), BF16),
            pltpu.VMEM((DATES, XS, SETS, rows), BF16),
            pltpu.VMEM((scen_n, 1, DATES * SETS), F32),
            dma((2, zs)),
            dma((2, zs)),
            dma((2, XS, 2)),
            dma((2, XS, 2)),
            dma((DATES, 2, zs // 2 + 1, P_CUTS)),
            dma((DATES, 2, zs // 2 + 1, P_CUTS)),
            dma((2, ys // 2 + 1, M_CUTS)),
            dma((2, ys // 2 + 1, M_CUTS)),
            dma((2, ys // 2 + 1, M_CUTS)),
            dma((2, ys // 2 + 1, M_CUTS)),
            dma((DATES, XS)),
            dma((DATES, XS)),
            dma((scen_n,)),
            dma((scen_n,)),
        ],
        compiler_params=pltpu.CompilerParams(
            collective_id=0, has_side_effects=True, vmem_limit_bytes=60 * 1024 * 1024
        ),
    )(*arrays)


def solution(mesh):
    placed = (
        P(None, "scen", None),
        P(None, "fac"),
        P("fac"),
        P(None, "scen", "fac"),
        P(None, "scen", "fac"),
        P("fac"),
        P("fac"),
        P("fac", None),
        P(),
        P("fac", None, None),
        P("fac"),
    )
    return jax.shard_map(
        body,
        mesh=mesh,
        in_specs=placed,
        out_specs=(P(None, "fac", "scen"), P(None, "fac")),
        check_vma=False,
    )
```

```python
import functools

import jax
import jax.numpy as jnp
from jax import lax
from jax.experimental import pallas as pl
from jax.experimental.pallas import tpu as pltpu
from jax.sharding import PartitionSpec as P

BLOCK = 128
SETS = 64
DATES = 2
CORES = 2
XS = 4
P_CUTS = 2
M_CUTS = 2
MESH = pl.DeviceIdType.MESH
F32 = jnp.float32
BF16 = jnp.bfloat16
NT = (((1,), (1,)), ((), ()))
INPUTS = 11
FIRST = (8, 7, 10, 9)
LATER = (0, 1, 3, 4, 2, 5, 6)


class Ring:
    def __init__(self, n, me, axis, device, view, send, recv, cuts, hops):
        self.n, self.me, self.axis, self.device, self.view = n, me, axis, device, view
        self.send, self.recv, self.cuts, self.hops = send, recv, cuts, hops
        self.last = n // 2

    def pieces(self, way, d):
        half = self.cuts // 2
        if d < self.last:
            return range(self.cuts)
        return range(way * half, (way + 1) * half)

    def owner(self, way, d):
        step = -d if way == 0 else d
        return lax.rem(self.me + step + self.n, self.n)

    def copy(self, way, d, piece, shift):
        ref = self.view(self.owner(way, d - shift), piece)
        to = self.owner(way, -self.hops[d])
        return pltpu.make_async_remote_copy(
            src_ref=ref,
            dst_ref=ref,
            send_sem=self.send.at[way, d, piece],
            recv_sem=self.recv.at[way, d, piece],
            device_id={self.axis: self.device(to)},
            device_id_type=MESH,
        )

    def start(self, way, d, piece):
        self.copy(way, d, piece, self.hops[d]).start()

    def begin(self):
        for piece in range(self.cuts):
            for d in range(self.last, 0, -1):
                for way in range(2):
                    if d == self.hops[d] and piece in self.pieces(way, d):
                        self.start(way, d, piece)

    def step(self, d, also=None, only=None):
        if d > self.last:
            return
        for piece in range(self.cuts) if only is None else (only,):
            for way in range(2):
                if piece in self.pieces(way, d):
                    self.copy(way, d, piece, 0).wait_recv()
                    for later in range(d + 1, self.last + 1):
                        if later - self.hops[later] == d and piece in self.pieces(way, later):
                            self.start(way, later, piece)
                    if also is not None:
                        also(way, d, piece)

    def sent(self):
        for d in range(1, self.last + 1):
            for way in range(2):
                for piece in self.pieces(way, d):
                    self.copy(way, d, piece, self.hops[d]).wait_send()


def kernel(
    fac_n,
    scen_n,
    *refs,
):
    given, refs = refs[:INPUTS], refs[INPUTS:]
    expo, mean, *refs = refs
    held, refs = refs[:INPUTS], refs[INPUTS:]
    run(fac_n, scen_n, given, held, expo, mean, *refs)


def run(
    fac_n,
    scen_n,
    given,
    held,
    expo,
    mean,
    load_sem,
    w32,
    keys,
    wg,
    marks,
    spread,
    macc,
    mg,
    level,
    pg,
    nets,
    part,
    back,
    sums,
    z_send,
    z_recv,
    x_send,
    x_recv,
    p_send,
    p_recv,
    m_send,
    m_recv,
    c_send,
    c_recv,
    r_send,
    r_recv,
    s_send,
    s_recv,
):
    loads = [
        pltpu.make_async_copy(src, dst, load_sem.at[i])
        for i, (src, dst) in enumerate(zip(given, held))
    ]
    for i in FIRST:
        loads[i].start()
    for i in LATER:
        loads[i].start()
    (shocks, loadings, vol, counts, noise, jump_mean, jump_vol, deps, place, weights, netting) = (
        held
    )
    zs = fac_n // XS
    ys = scen_n // CORES
    rows = shocks.shape[1]
    width = loadings.shape[1]
    local = width // BLOCK
    trades = netting.shape[1]
    jn = BLOCK // scen_n
    fac = lax.axis_index("fac")
    scen = lax.axis_index("scen")
    z, x = fac // XS, lax.rem(fac, XS)
    y, c = scen // CORES, lax.rem(scen, CORES)

    barrier = pltpu.get_barrier_semaphore()
    partners = 0
    for d in range(1, zs):
        pl.semaphore_signal(
            barrier, inc=1, device_id={"fac": lax.rem(z + d, zs) * XS + x}, device_id_type=MESH
        )
        partners += 1
    for d in range(1, XS):
        pl.semaphore_signal(
            barrier, inc=1, device_id={"fac": z * XS + lax.rem(x + d, XS)}, device_id_type=MESH
        )
        partners += 1
    for d in range(1, scen_n):
        pl.semaphore_signal(
            barrier, inc=1, device_id={"scen": lax.rem(scen + d, scen_n)}, device_id_type=MESH
        )
        partners += 1

    for i in FIRST:
        loads[i].wait()

    dep = deps[...]
    slot = jnp.zeros_like(dep)
    for b in range(place.shape[0]):
        slot = jnp.where(dep == b, place[b], slot)
    keys[x, 0, :, 0:trades] = slot[0:1]
    keys[x, 0, :, trades : 2 * trades] = slot[1:2]
    keys[x, 0, :, 2 * trades : 3 * trades] = netting[...]
    w32[...] = weights[...].astype(F32)
    pick = (
        lax.broadcasted_iota(jnp.int32, (jn, BLOCK), 1)
        == lax.broadcasted_iota(jnp.int32, (jn, BLOCK), 0) + scen * jn
    ).astype(F32).astype(BF16)
    chosen = [
        lax.dot_general(
            pick, w32[pl.ds(k, trades, stride=2), :].astype(BF16), NT, preferred_element_type=F32
        )
        for k in range(2)
    ]
    wg[x, 0] = jnp.concatenate(chosen, axis=0).astype(BF16)

    near = [0]
    for d in range(1, zs // 2 + 1):
        near += [d] if 2 * d == zs else [d, zs - d]
    cut = zs * 5 // 8
    groups = ((0, cut), (cut, zs))

    def z_copy(kind, d):
        buffer = keys if kind == 0 else wg
        return pltpu.make_async_remote_copy(
            src_ref=buffer.at[x, 0],
            dst_ref=buffer.at[x, near.index(d)],
            send_sem=z_send.at[kind, d],
            recv_sem=z_recv.at[kind, d],
            device_id={"fac": lax.rem(z + d, zs) * XS + x},
            device_id_type=MESH,
        )

    def x_copy(kind, d, piece, from_x):
        buffer = keys if kind == 0 else wg
        low, high = groups[piece]
        ref = buffer.at[from_x, pl.ds(low, high - low)]
        return pltpu.make_async_remote_copy(
            src_ref=ref,
            dst_ref=ref,
            send_sem=x_send.at[kind, d, piece],
            recv_sem=x_recv.at[kind, d, piece],
            device_id={"fac": z * XS + lax.rem(x + d, XS)},
            device_id_type=MESH,
        )

    pl.semaphore_wait(barrier, partners)
    for d in near[:0:-1]:
        for kind in range(2):
            z_copy(kind, d).start()
    for i in LATER:
        loads[i].wait()

    p_rings = []
    cut_rows = rows // P_CUTS
    for date in range(DATES):

        def p_view(owner, piece, date=date):
            return pg.at[date, owner, pl.ds(piece * cut_rows, cut_rows)]

        p_rings.append(
            Ring(
                zs,
                z,
                "fac",
                lambda i: i * XS + x,
                p_view,
                p_send.at[date],
                p_recv.at[date],
                P_CUTS,
                (0, 1, 1, 1, 1),
            )
        )

    col_q = lax.broadcasted_iota(jnp.int32, (width, width), 1)
    col_f = (
        lax.rem(lax.div(col_q, jn), local) * BLOCK
        + lax.div(col_q, jn * local) * jn
        + lax.rem(col_q, jn)
    )
    perm = (lax.broadcasted_iota(jnp.int32, (width, width), 0) == col_f).astype(F32).astype(BF16)
    v = vol[...]
    drift = 0.5 * v * v
    for date in range(DATES):
        diffuse = jnp.dot(shocks[date], loadings[...], preferred_element_type=F32)
        number = counts[date].astype(F32)
        change = (
            v * diffuse
            - drift
            + number * jump_mean[...]
            + jnp.sqrt(number) * jump_vol[...] * noise[date].astype(F32)
        )
        now = change if date == 0 else level[...] + change
        if date < DATES - 1:
            level[...] = now
        prices = (jnp.exp(now) - 1.0).astype(BF16)
        pg[date, z] = jnp.dot(prices, perm, preferred_element_type=F32).astype(BF16)
        p_rings[date].begin()

    sets = XS * SETS
    part_sets = SETS // M_CUTS
    macc[...] = jnp.zeros_like(macc)

    def form(owner, piece):
        low, high = groups[piece]

        @pl.loop(low, high)
        def _(at):
            columns = pl.ds(pl.multiple_of(at * trades, trades), trades)
            key = keys[owner, at]
            net = key[:, 2 * trades : 3 * trades] - sets * z
            line = jnp.where(
                (net >= 0) & (net < sets),
                lax.div(lax.rem(net, SETS), part_sets) * (XS * part_sets)
                + lax.div(net, SETS) * part_sets
                + lax.rem(net, part_sets),
                -1,
            )
            marks[:, columns] = jnp.where(
                lax.broadcasted_iota(jnp.int32, (sets, trades), 0) == line, 1.0, 0.0
            ).astype(BF16)
            w = wg[owner, at].astype(F32)
            w0, w1 = w[0:jn], w[jn : 2 * jn]
            first = key[:, 0:trades] - local * x
            second = key[:, trades : 2 * trades] - local * x
            spread[:, columns] = jnp.concatenate(
                [
                    jnp.where(first == b, w0, 0.0) + jnp.where(second == b, w1, 0.0)
                    for b in [
                        to_z * XS * local + of for to_z in range(zs) for of in range(local)
                    ]
                ],
                axis=0,
            ).astype(BF16)

        columns = pl.ds(low * trades, (high - low) * trades)
        macc[...] += lax.dot_general(
            spread[:, columns], marks[:, columns], NT, preferred_element_type=F32
        )

    def form_from(d, piece):
        from_x = lax.rem(x - d + XS, XS)
        for kind in range(2):
            x_copy(kind, d, piece, from_x).wait_recv()
        form(from_x, piece)

    for piece, (low, high) in enumerate(groups):
        for d in near[max(low, 1) : high]:
            for kind in range(2):
                z_copy(kind, d).wait_recv()
        for d in (2, 1, XS - 1):
            for kind in range(2):
                x_copy(kind, d, piece, x).start()
        if piece == 1:
            p_rings[0].step(1)
        form(x, piece)
    p_rings[1].step(1)
    form_from(1, 0)
    form_from(XS - 1, 0)
    form_from(2, 0)
    p_rings[0].step(2)
    form_from(1, 1)
    form_from(XS - 1, 1)
    p_rings[1].step(2)
    form_from(2, 1)
    mg[scen] = macc[...].astype(BF16)

    cut_sets = sets // M_CUTS

    def m_view(core):
        def view(owner, piece):
            return mg.at[owner * CORES + core, :, pl.ds(piece * cut_sets, cut_sets)]

        return view

    m_ring = Ring(
        ys,
        y,
        "scen",
        lambda i: i * CORES + c,
        m_view(c),
        m_send,
        m_recv,
        M_CUTS,
        (0, 1, 2, 1, 2),
    )
    other = 1 - c

    def c_copy(way, d, piece, core):
        ref = m_view(core)(m_ring.owner(way, d), piece)
        return pltpu.make_async_remote_copy(
            src_ref=ref,
            dst_ref=ref,
            send_sem=c_send.at[way, d, piece],
            recv_sem=c_recv.at[way, d, piece],
            device_id={"scen": y * CORES + other},
            device_id_type=MESH,
        )

    def pass_on(way, d, piece):
        c_copy(way, d, piece, c).start()

    c_pieces = [(0, 0, piece) for piece in range(M_CUTS)] + [
        (way, d, piece)
        for d in range(1, ys // 2 + 1)
        for way in range(2)
        for piece in m_ring.pieces(way, d)
    ]
    m_ring.begin()
    for piece in range(M_CUTS):
        pass_on(0, 0, piece)
    for ring in p_rings:
        ring.step(3)
    for piece in range(M_CUTS):
        m_ring.step(2, pass_on, piece)
        m_ring.step(1, pass_on, piece)
    p_rings[0].step(4)

    def r_copy(date, d, piece, to):
        return pltpu.make_async_remote_copy(
            src_ref=part.at[date, piece, to],
            dst_ref=back.at[date, piece, d],
            send_sem=r_send.at[date, piece, d],
            recv_sem=r_recv.at[date, piece, d],
            device_id={"fac": z * XS + lax.rem(x + d, XS)},
            device_id_type=MESH,
        )

    tall = local * jn
    for piece in range(M_CUTS):
        m_ring.step(3, pass_on, piece)
        m_ring.step(4, pass_on, piece)
        if piece == 0:
            p_rings[1].step(4)
        for way, d, at in c_pieces:
            if at == piece:
                c_copy(way, d, at, other).wait_recv()
        for date in range(DATES):
            total = None
            for at in range(zs):
                term = jnp.dot(
                    pg[date, at],
                    mg[
                        :,
                        at * tall : (at + 1) * tall,
                        piece * cut_sets : (piece + 1) * cut_sets,
                    ].reshape(scen_n * tall, cut_sets),
                    preferred_element_type=F32,
                )
                total = term if total is None else total + term
            turned = total.T.reshape(XS, part_sets, rows)
            nets[date, piece] = turned
            part[date, piece] = turned.astype(BF16)
            for d in (2, 1, XS - 1):
                r_copy(date, d, piece, lax.rem(x + d, XS)).start()
    for piece in range(M_CUTS):
        for date in range(DATES):
            total = nets[date, piece, x]
            for d in (1, XS - 1, 2):
                r_copy(date, d, piece, 0).wait_recv()
                total = total + back[date, piece, d].astype(F32)
            expo[date, piece * part_sets : (piece + 1) * part_sets] = jnp.maximum(total, 0.0)

    both = jnp.concatenate([expo[date] for date in range(DATES)], axis=0)
    high = both.astype(BF16)
    low = (both - high.astype(F32)).astype(BF16)
    row = lax.dot_general(
        jnp.ones((8, 2 * rows), BF16),
        jnp.concatenate([high, low], axis=1),
        NT,
        preferred_element_type=F32,
    )
    sums[0] = row[0:1]

    def s_copy(d):
        return pltpu.make_async_remote_copy(
            src_ref=sums.at[0],
            dst_ref=sums.at[d],
            send_sem=s_send.at[d],
            recv_sem=s_recv.at[d],
            device_id={"scen": lax.rem(scen + d, scen_n)},
            device_id_type=MESH,
        )

    for d in range(1, scen_n):
        s_copy(d).start()
    for d in range(1, scen_n):
        s_copy(d).wait_recv()
    average = jnp.sum(sums[...], axis=0) / (rows * scen_n)
    for date in range(DATES):
        mean[date : date + 1, :] = average[:, date * SETS : (date + 1) * SETS]

    for kind in range(2):
        for d in range(1, zs):
            z_copy(kind, d).wait_send()
        for d in range(1, XS):
            for piece in range(2):
                x_copy(kind, d, piece, x).wait_send()
    for ring in p_rings:
        ring.sent()
    m_ring.sent()
    for way, d, piece in c_pieces:
        c_copy(way, d, piece, c).wait_send()
    for date in range(DATES):
        for d in range(1, XS):
            for piece in range(M_CUTS):
                r_copy(date, d, piece, 0).wait_send()
    for d in range(1, scen_n):
        s_copy(d).wait_send()


def body(
    shocks,
    loadings,
    vol,
    jump_counts,
    jump_noise,
    jump_mean,
    jump_vol,
    dependencies,
    block_slot,
    trade_weights,
    netting,
):
    fac_n = lax.axis_size("fac")
    scen_n = lax.axis_size("scen")
    zs = fac_n // XS
    ys = scen_n // CORES
    rows = shocks.shape[1]
    width = loadings.shape[1]
    trades = netting.shape[0]
    local = width // BLOCK
    jn = BLOCK // scen_n
    tall = zs * local * jn
    sets = XS * SETS
    vmem = pl.BlockSpec(memory_space=pltpu.VMEM)
    hbm = pl.BlockSpec(memory_space=pltpu.HBM)
    dma = pltpu.SemaphoreType.DMA
    arrays = (
        shocks,
        loadings,
        vol.reshape(1, width),
        jump_counts,
        jump_noise,
        jump_mean.reshape(1, width),
        jump_vol.reshape(1, width),
        dependencies.T,
        block_slot,
        trade_weights.reshape(2 * trades, BLOCK),
        netting.reshape(1, trades),
    )
    return pl.pallas_call(
        functools.partial(kernel, fac_n, scen_n),
        out_shape=(
            jax.ShapeDtypeStruct((DATES, SETS, rows), F32),
            jax.ShapeDtypeStruct((DATES, SETS), F32),
        ),
        in_specs=[hbm] * INPUTS,
        out_specs=(vmem, vmem),
        scratch_shapes=[
            (pltpu.SMEM if i == 8 else pltpu.VMEM)(a.shape, a.dtype) for i, a in enumerate(arrays)
        ]
        + [
            dma((INPUTS,)),
            pltpu.VMEM((2 * trades, BLOCK), F32),
            pltpu.VMEM((XS, zs, 1, 3 * trades), jnp.int32),
            pltpu.VMEM((XS, zs, 2 * jn, trades), BF16),
            pltpu.VMEM((sets, zs * trades), BF16),
            pltpu.VMEM((tall, zs * trades), BF16),
            pltpu.VMEM((tall, sets), F32),
            pltpu.VMEM((scen_n, tall, sets), BF16),
            pltpu.VMEM((rows, width), F32),
            pltpu.VMEM((DATES, zs, rows, width), BF16),
            pltpu.VMEM((DATES, M_CUTS, XS, SETS // M_CUTS, rows), F32),
            pltpu.VMEM((DATES, M_CUTS, XS, SETS // M_CUTS, rows), BF16),
            pltpu.VMEM((DATES, M_CUTS, XS, SETS // M_CUTS, rows), BF16),
            pltpu.VMEM((scen_n, 1, DATES * SETS), F32),
            dma((2, zs)),
            dma((2, zs)),
            dma((2, XS, 2)),
            dma((2, XS, 2)),
            dma((DATES, 2, zs // 2 + 1, P_CUTS)),
            dma((DATES, 2, zs // 2 + 1, P_CUTS)),
            dma((2, ys // 2 + 1, M_CUTS)),
            dma((2, ys // 2 + 1, M_CUTS)),
            dma((2, ys // 2 + 1, M_CUTS)),
            dma((2, ys // 2 + 1, M_CUTS)),
            dma((DATES, M_CUTS, XS)),
            dma((DATES, M_CUTS, XS)),
            dma((scen_n,)),
            dma((scen_n,)),
        ],
        compiler_params=pltpu.CompilerParams(
            collective_id=0, has_side_effects=True, vmem_limit_bytes=60 * 1024 * 1024
        ),
    )(*arrays)


def solution(mesh):
    placed = (
        P(None, "scen", None),
        P(None, "fac"),
        P("fac"),
        P(None, "scen", "fac"),
        P(None, "scen", "fac"),
        P("fac"),
        P("fac"),
        P("fac", None),
        P(),
        P("fac", None, None),
        P("fac"),
    )
    return jax.shard_map(
        body,
        mesh=mesh,
        in_specs=placed,
        out_specs=(P(None, "fac", "scen"), P(None, "fac")),
        check_vma=False,
    )
```

```python
import functools

import jax
import jax.numpy as jnp
from jax import lax
from jax.experimental import pallas as pl
from jax.experimental.pallas import tpu as pltpu
from jax.sharding import PartitionSpec as P

BLOCK = 128
SETS = 64
DATES = 2
CORES = 2
XS = 4
P_CUTS = 2
M_CUTS = 2
MESH = pl.DeviceIdType.MESH
F32 = jnp.float32
BF16 = jnp.bfloat16
NT = (((1,), (1,)), ((), ()))
INPUTS = 11
FIRST = (8, 7, 10, 9)
LATER = (0, 1, 3, 4, 2, 5, 6)


class Ring:
    def __init__(self, n, me, axis, device, view, send, recv, cuts, hops):
        self.n, self.me, self.axis, self.device, self.view = n, me, axis, device, view
        self.send, self.recv, self.cuts, self.hops = send, recv, cuts, hops
        self.last = n // 2

    def pieces(self, way, d):
        half = self.cuts // 2
        if d < self.last:
            return range(self.cuts)
        return range(way * half, (way + 1) * half)

    def owner(self, way, d):
        step = -d if way == 0 else d
        return lax.rem(self.me + step + self.n, self.n)

    def copy(self, way, d, piece, shift):
        ref = self.view(self.owner(way, d - shift), piece)
        to = self.owner(way, -self.hops[d])
        return pltpu.make_async_remote_copy(
            src_ref=ref,
            dst_ref=ref,
            send_sem=self.send.at[way, d, piece],
            recv_sem=self.recv.at[way, d, piece],
            device_id={self.axis: self.device(to)},
            device_id_type=MESH,
        )

    def start(self, way, d, piece):
        self.copy(way, d, piece, self.hops[d]).start()

    def begin(self):
        for d in range(self.last, 0, -1):
            for piece in range(self.cuts):
                for way in range(2):
                    if d == self.hops[d] and piece in self.pieces(way, d):
                        self.start(way, d, piece)

    def step(self, d, also=None):
        if d > self.last:
            return
        for piece in range(self.cuts):
            for way in range(2):
                if piece in self.pieces(way, d):
                    self.copy(way, d, piece, 0).wait_recv()
                    for later in range(d + 1, self.last + 1):
                        if later - self.hops[later] == d and piece in self.pieces(way, later):
                            self.start(way, later, piece)
                    if also is not None:
                        also(way, d, piece)

    def sent(self):
        for d in range(1, self.last + 1):
            for way in range(2):
                for piece in self.pieces(way, d):
                    self.copy(way, d, piece, self.hops[d]).wait_send()


def kernel(
    fac_n,
    scen_n,
    *refs,
):
    given, refs = refs[:INPUTS], refs[INPUTS:]
    expo, mean, *refs = refs
    held, refs = refs[:INPUTS], refs[INPUTS:]
    run(fac_n, scen_n, given, held, expo, mean, *refs)


def run(
    fac_n,
    scen_n,
    given,
    held,
    expo,
    mean,
    load_sem,
    w32,
    keys,
    wg,
    marks,
    spread,
    macc,
    mg,
    level,
    pg,
    nets,
    part,
    back,
    sums,
    z_send,
    z_recv,
    x_send,
    x_recv,
    p_send,
    p_recv,
    m_send,
    m_recv,
    c_send,
    c_recv,
    r_send,
    r_recv,
    s_send,
    s_recv,
):
    loads = [
        pltpu.make_async_copy(src, dst, load_sem.at[i])
        for i, (src, dst) in enumerate(zip(given, held))
    ]
    for i in FIRST:
        loads[i].start()
    for i in LATER:
        loads[i].start()
    (shocks, loadings, vol, counts, noise, jump_mean, jump_vol, deps, place, weights, netting) = (
        held
    )
    zs = fac_n // XS
    ys = scen_n // CORES
    rows = shocks.shape[1]
    width = loadings.shape[1]
    local = width // BLOCK
    trades = netting.shape[1]
    jn = BLOCK // scen_n
    fac = lax.axis_index("fac")
    scen = lax.axis_index("scen")
    z, x = fac // XS, lax.rem(fac, XS)
    y, c = scen // CORES, lax.rem(scen, CORES)

    barrier = pltpu.get_barrier_semaphore()
    partners = 0
    for d in range(1, zs):
        pl.semaphore_signal(
            barrier, inc=1, device_id={"fac": lax.rem(z + d, zs) * XS + x}, device_id_type=MESH
        )
        partners += 1
    for d in range(1, XS):
        pl.semaphore_signal(
            barrier, inc=1, device_id={"fac": z * XS + lax.rem(x + d, XS)}, device_id_type=MESH
        )
        partners += 1
    for d in range(1, scen_n):
        pl.semaphore_signal(
            barrier, inc=1, device_id={"scen": lax.rem(scen + d, scen_n)}, device_id_type=MESH
        )
        partners += 1

    for i in FIRST:
        loads[i].wait()

    dep = deps[...]
    slot = jnp.zeros_like(dep)
    for b in range(place.shape[0]):
        slot = jnp.where(dep == b, place[b], slot)
    keys[x, 0, :, 0:trades] = slot[0:1]
    keys[x, 0, :, trades : 2 * trades] = slot[1:2]
    keys[x, 0, :, 2 * trades : 3 * trades] = netting[...]
    w32[...] = weights[...].astype(F32)
    pick = (
        lax.broadcasted_iota(jnp.int32, (jn, BLOCK), 1)
        == lax.broadcasted_iota(jnp.int32, (jn, BLOCK), 0) + scen * jn
    ).astype(F32).astype(BF16)
    chosen = [
        lax.dot_general(
            pick, w32[pl.ds(k, trades, stride=2), :].astype(BF16), NT, preferred_element_type=F32
        )
        for k in range(2)
    ]
    wg[x, 0] = jnp.concatenate(chosen, axis=0).astype(BF16)

    near = [0]
    for d in range(1, zs // 2 + 1):
        near += [d] if 2 * d == zs else [d, zs - d]
    cut = zs * 5 // 8
    groups = ((0, cut), (cut, zs))

    def z_copy(kind, d):
        buffer = keys if kind == 0 else wg
        return pltpu.make_async_remote_copy(
            src_ref=buffer.at[x, 0],
            dst_ref=buffer.at[x, near.index(d)],
            send_sem=z_send.at[kind, d],
            recv_sem=z_recv.at[kind, d],
            device_id={"fac": lax.rem(z + d, zs) * XS + x},
            device_id_type=MESH,
        )

    def x_copy(kind, d, piece, from_x):
        buffer = keys if kind == 0 else wg
        low, high = groups[piece]
        ref = buffer.at[from_x, pl.ds(low, high - low)]
        return pltpu.make_async_remote_copy(
            src_ref=ref,
            dst_ref=ref,
            send_sem=x_send.at[kind, d, piece],
            recv_sem=x_recv.at[kind, d, piece],
            device_id={"fac": z * XS + lax.rem(x + d, XS)},
            device_id_type=MESH,
        )

    pl.semaphore_wait(barrier, partners)
    for d in near[:0:-1]:
        for kind in range(2):
            z_copy(kind, d).start()
    for i in LATER:
        loads[i].wait()

    p_rings = []
    cut_rows = rows // P_CUTS
    for date in range(DATES):

        def p_view(owner, piece, date=date):
            return pg.at[date, owner, pl.ds(piece * cut_rows, cut_rows)]

        p_rings.append(
            Ring(
                zs,
                z,
                "fac",
                lambda i: i * XS + x,
                p_view,
                p_send.at[date],
                p_recv.at[date],
                P_CUTS,
                (0, 1, 1, 1, 1),
            )
        )

    col_q = lax.broadcasted_iota(jnp.int32, (width, width), 1)
    col_f = (
        lax.rem(lax.div(col_q, jn), local) * BLOCK
        + lax.div(col_q, jn * local) * jn
        + lax.rem(col_q, jn)
    )
    perm = (lax.broadcasted_iota(jnp.int32, (width, width), 0) == col_f).astype(F32).astype(BF16)
    v = vol[...]
    drift = 0.5 * v * v
    for date in range(DATES):
        diffuse = jnp.dot(shocks[date], loadings[...], preferred_element_type=F32)
        number = counts[date].astype(F32)
        change = (
            v * diffuse
            - drift
            + number * jump_mean[...]
            + jnp.sqrt(number) * jump_vol[...] * noise[date].astype(F32)
        )
        now = change if date == 0 else level[...] + change
        if date < DATES - 1:
            level[...] = now
        prices = (jnp.exp(now) - 1.0).astype(BF16)
        pg[date, z] = jnp.dot(prices, perm, preferred_element_type=F32).astype(BF16)
        p_rings[date].begin()

    sets = XS * SETS
    macc[...] = jnp.zeros_like(macc)

    def form(owner, piece):
        low, high = groups[piece]

        @pl.loop(low, high)
        def _(at):
            columns = pl.ds(pl.multiple_of(at * trades, trades), trades)
            key = keys[owner, at]
            line = key[:, 2 * trades : 3 * trades] - sets * z
            marks[:, columns] = jnp.where(
                lax.broadcasted_iota(jnp.int32, (sets, trades), 0) == line, 1.0, 0.0
            ).astype(BF16)
            w = wg[owner, at].astype(F32)
            w0, w1 = w[0:jn], w[jn : 2 * jn]
            first = key[:, 0:trades] - local * x
            second = key[:, trades : 2 * trades] - local * x
            spread[:, columns] = jnp.concatenate(
                [
                    jnp.where(first == b, w0, 0.0) + jnp.where(second == b, w1, 0.0)
                    for b in [
                        to_z * XS * local + of for to_z in range(zs) for of in range(local)
                    ]
                ],
                axis=0,
            ).astype(BF16)

        columns = pl.ds(low * trades, (high - low) * trades)
        macc[...] += lax.dot_general(
            spread[:, columns], marks[:, columns], NT, preferred_element_type=F32
        )

    def form_from(d, piece):
        from_x = lax.rem(x - d + XS, XS)
        for kind in range(2):
            x_copy(kind, d, piece, from_x).wait_recv()
        form(from_x, piece)

    for piece, (low, high) in enumerate(groups):
        for d in near[max(low, 1) : high]:
            for kind in range(2):
                z_copy(kind, d).wait_recv()
        for d in (2, 1, XS - 1):
            for kind in range(2):
                x_copy(kind, d, piece, x).start()
        if piece == 1:
            p_rings[0].step(1)
        form(x, piece)
    form_from(1, 0)
    form_from(XS - 1, 0)
    form_from(2, 0)
    p_rings[1].step(1)
    form_from(1, 1)
    form_from(XS - 1, 1)
    form_from(2, 1)
    mg[scen] = macc[...].astype(BF16)

    cut_tall = macc.shape[0] // M_CUTS

    def m_view(core):
        def view(owner, piece):
            return mg.at[owner * CORES + core, pl.ds(piece * cut_tall, cut_tall)]

        return view

    m_ring = Ring(
        ys,
        y,
        "scen",
        lambda i: i * CORES + c,
        m_view(c),
        m_send,
        m_recv,
        M_CUTS,
        (0, 1, 2, 1, 2),
    )
    other = 1 - c

    def c_copy(way, d, piece, core):
        ref = m_view(core)(m_ring.owner(way, d), piece)
        return pltpu.make_async_remote_copy(
            src_ref=ref,
            dst_ref=ref,
            send_sem=c_send.at[way, d, piece],
            recv_sem=c_recv.at[way, d, piece],
            device_id={"scen": y * CORES + other},
            device_id_type=MESH,
        )

    def pass_on(way, d, piece):
        c_copy(way, d, piece, c).start()

    c_pieces = [(0, 0, piece) for piece in range(M_CUTS)] + [
        (way, d, piece)
        for d in range(1, ys // 2 + 1)
        for way in range(2)
        for piece in m_ring.pieces(way, d)
    ]
    m_ring.begin()
    for piece in range(M_CUTS):
        pass_on(0, 0, piece)
    p_rings[0].step(2)
    p_rings[1].step(2)
    m_ring.step(2, pass_on)
    p_rings[0].step(3)
    m_ring.step(1, pass_on)
    p_rings[1].step(3)
    m_ring.step(3, pass_on)
    m_ring.step(4, pass_on)
    for way, d, piece in c_pieces:
        c_copy(way, d, piece, other).wait_recv()

    def r_copy(date, d, slot_at):
        return pltpu.make_async_remote_copy(
            src_ref=part.at[date, slot_at],
            dst_ref=back.at[date, d],
            send_sem=r_send.at[date, d],
            recv_sem=r_recv.at[date, d],
            device_id={"fac": z * XS + lax.rem(x + d, XS)},
            device_id_type=MESH,
        )

    tall = local * jn
    for date in range(DATES):
        p_rings[date].step(4)
        total = None
        for at in range(zs):
            term = jnp.dot(
                pg[date, at],
                mg[:, at * tall : (at + 1) * tall, :].reshape(scen_n * tall, sets),
                preferred_element_type=F32,
            )
            total = term if total is None else total + term
        turned = total.T.reshape(XS, SETS, rows)
        nets[date] = turned
        part[date] = turned.astype(BF16)
        for d in (1, XS - 1, 2):
            r_copy(date, d, lax.rem(x + d, XS)).start()
    for date in range(DATES):
        total = nets[date, x]
        for d in (1, XS - 1, 2):
            r_copy(date, d, 0).wait_recv()
            total = total + back[date, d].astype(F32)
        expo[date] = jnp.maximum(total, 0.0)

    both = jnp.concatenate([expo[date] for date in range(DATES)], axis=0)
    high = both.astype(BF16)
    low = (both - high.astype(F32)).astype(BF16)
    row = lax.dot_general(
        jnp.ones((8, 2 * rows), BF16),
        jnp.concatenate([high, low], axis=1),
        NT,
        preferred_element_type=F32,
    )
    sums[0] = row[0:1]

    def s_copy(d):
        return pltpu.make_async_remote_copy(
            src_ref=sums.at[0],
            dst_ref=sums.at[d],
            send_sem=s_send.at[d],
            recv_sem=s_recv.at[d],
            device_id={"scen": lax.rem(scen + d, scen_n)},
            device_id_type=MESH,
        )

    for d in sorted(range(1, scen_n), key=lambda d: -min(d, scen_n - d)):
        s_copy(d).start()
    for kind in range(2):
        for d in range(1, zs):
            z_copy(kind, d).wait_send()
        for d in range(1, XS):
            for piece in range(2):
                x_copy(kind, d, piece, x).wait_send()
    for ring in p_rings:
        ring.sent()
    m_ring.sent()
    for way, d, piece in c_pieces:
        c_copy(way, d, piece, c).wait_send()
    for date in range(DATES):
        for d in range(1, XS):
            r_copy(date, d, 0).wait_send()
    for d in range(1, scen_n):
        s_copy(d).wait_recv()
    average = jnp.sum(sums[...], axis=0) / (rows * scen_n)
    for date in range(DATES):
        mean[date : date + 1, :] = average[:, date * SETS : (date + 1) * SETS]

    for d in range(1, scen_n):
        s_copy(d).wait_send()


def body(
    shocks,
    loadings,
    vol,
    jump_counts,
    jump_noise,
    jump_mean,
    jump_vol,
    dependencies,
    block_slot,
    trade_weights,
    netting,
):
    fac_n = lax.axis_size("fac")
    scen_n = lax.axis_size("scen")
    zs = fac_n // XS
    ys = scen_n // CORES
    rows = shocks.shape[1]
    width = loadings.shape[1]
    trades = netting.shape[0]
    local = width // BLOCK
    jn = BLOCK // scen_n
    tall = zs * local * jn
    sets = XS * SETS
    vmem = pl.BlockSpec(memory_space=pltpu.VMEM)
    hbm = pl.BlockSpec(memory_space=pltpu.HBM)
    dma = pltpu.SemaphoreType.DMA
    arrays = (
        shocks,
        loadings,
        vol.reshape(1, width),
        jump_counts,
        jump_noise,
        jump_mean.reshape(1, width),
        jump_vol.reshape(1, width),
        dependencies.T,
        block_slot,
        trade_weights.reshape(2 * trades, BLOCK),
        netting.reshape(1, trades),
    )
    return pl.pallas_call(
        functools.partial(kernel, fac_n, scen_n),
        out_shape=(
            jax.ShapeDtypeStruct((DATES, SETS, rows), F32),
            jax.ShapeDtypeStruct((DATES, SETS), F32),
        ),
        in_specs=[hbm] * INPUTS,
        out_specs=(vmem, vmem),
        scratch_shapes=[
            (pltpu.SMEM if i == 8 else pltpu.VMEM)(a.shape, a.dtype) for i, a in enumerate(arrays)
        ]
        + [
            dma((INPUTS,)),
            pltpu.VMEM((2 * trades, BLOCK), F32),
            pltpu.VMEM((XS, zs, 1, 3 * trades), jnp.int32),
            pltpu.VMEM((XS, zs, 2 * jn, trades), BF16),
            pltpu.VMEM((sets, zs * trades), BF16),
            pltpu.VMEM((tall, zs * trades), BF16),
            pltpu.VMEM((tall, sets), F32),
            pltpu.VMEM((scen_n, tall, sets), BF16),
            pltpu.VMEM((rows, width), F32),
            pltpu.VMEM((DATES, zs, rows, width), BF16),
            pltpu.VMEM((DATES, XS, SETS, rows), F32),
            pltpu.VMEM((DATES, XS, SETS, rows), BF16),
            pltpu.VMEM((DATES, XS, SETS, rows), BF16),
            pltpu.VMEM((scen_n, 1, DATES * SETS), F32),
            dma((2, zs)),
            dma((2, zs)),
            dma((2, XS, 2)),
            dma((2, XS, 2)),
            dma((DATES, 2, zs // 2 + 1, P_CUTS)),
            dma((DATES, 2, zs // 2 + 1, P_CUTS)),
            dma((2, ys // 2 + 1, M_CUTS)),
            dma((2, ys // 2 + 1, M_CUTS)),
            dma((2, ys // 2 + 1, M_CUTS)),
            dma((2, ys // 2 + 1, M_CUTS)),
            dma((DATES, XS)),
            dma((DATES, XS)),
            dma((scen_n,)),
            dma((scen_n,)),
        ],
        compiler_params=pltpu.CompilerParams(
            collective_id=0, has_side_effects=True, vmem_limit_bytes=60 * 1024 * 1024
        ),
    )(*arrays)


def solution(mesh):
    placed = (
        P(None, "scen", None),
        P(None, "fac"),
        P("fac"),
        P(None, "scen", "fac"),
        P(None, "scen", "fac"),
        P("fac"),
        P("fac"),
        P("fac", None),
        P(),
        P("fac", None, None),
        P("fac"),
    )
    return jax.shard_map(
        body,
        mesh=mesh,
        in_specs=placed,
        out_specs=(P(None, "fac", "scen"), P(None, "fac")),
        check_vma=False,
    )
```

```python
import functools

import jax
import jax.numpy as jnp
from jax import lax
from jax.experimental import pallas as pl
from jax.experimental.pallas import tpu as pltpu
from jax.sharding import PartitionSpec as P

BLOCK = 128
SETS = 64
DATES = 2
CORES = 2
XS = 4
P_CUTS = 2
M_CUTS = 2
MESH = pl.DeviceIdType.MESH
F32 = jnp.float32
BF16 = jnp.bfloat16
NT = (((1,), (1,)), ((), ()))
INPUTS = 11
FIRST = (8, 7, 10, 9)
LATER = (0, 1, 3, 4, 2, 5, 6)


class Ring:
    def __init__(self, n, me, axis, device, view, send, recv, cuts, hops):
        self.n, self.me, self.axis, self.device, self.view = n, me, axis, device, view
        self.send, self.recv, self.cuts, self.hops = send, recv, cuts, hops
        self.last = n // 2

    def pieces(self, way, d):
        half = self.cuts // 2
        if d < self.last:
            return range(self.cuts)
        return range(way * half, (way + 1) * half)

    def owner(self, way, d):
        step = -d if way == 0 else d
        return lax.rem(self.me + step + self.n, self.n)

    def copy(self, way, d, piece, shift):
        ref = self.view(self.owner(way, d - shift), piece)
        to = self.owner(way, -self.hops[d])
        return pltpu.make_async_remote_copy(
            src_ref=ref,
            dst_ref=ref,
            send_sem=self.send.at[way, d, piece],
            recv_sem=self.recv.at[way, d, piece],
            device_id={self.axis: self.device(to)},
            device_id_type=MESH,
        )

    def start(self, way, d, piece):
        self.copy(way, d, piece, self.hops[d]).start()

    def begin(self):
        for d in range(self.last, 0, -1):
            for piece in range(self.cuts):
                for way in range(2):
                    if d == self.hops[d] and piece in self.pieces(way, d):
                        self.start(way, d, piece)

    def step(self, d, also=None):
        if d > self.last:
            return
        for piece in range(self.cuts):
            for way in range(2):
                if piece in self.pieces(way, d):
                    self.copy(way, d, piece, 0).wait_recv()
                    for later in range(d + 1, self.last + 1):
                        if later - self.hops[later] == d and piece in self.pieces(way, later):
                            self.start(way, later, piece)
                    if also is not None:
                        also(way, d, piece)

    def sent(self):
        for d in range(1, self.last + 1):
            for way in range(2):
                for piece in self.pieces(way, d):
                    self.copy(way, d, piece, self.hops[d]).wait_send()


def kernel(
    fac_n,
    scen_n,
    *refs,
):
    given, refs = refs[:INPUTS], refs[INPUTS:]
    expo, mean, *refs = refs
    held, refs = refs[:INPUTS], refs[INPUTS:]
    run(fac_n, scen_n, given, held, expo, mean, *refs)


def run(
    fac_n,
    scen_n,
    given,
    held,
    expo,
    mean,
    load_sem,
    w32,
    keys,
    wg,
    marks,
    spread,
    macc,
    mg,
    level,
    pg,
    nets,
    part,
    back,
    sums,
    z_send,
    z_recv,
    x_send,
    x_recv,
    p_send,
    p_recv,
    m_send,
    m_recv,
    c_send,
    c_recv,
    r_send,
    r_recv,
    s_send,
    s_recv,
):
    loads = [
        pltpu.make_async_copy(src, dst, load_sem.at[i])
        for i, (src, dst) in enumerate(zip(given, held))
    ]
    for i in FIRST:
        loads[i].start()
    for i in LATER:
        loads[i].start()
    (shocks, loadings, vol, counts, noise, jump_mean, jump_vol, deps, place, weights, netting) = (
        held
    )
    zs = fac_n // XS
    ys = scen_n // CORES
    rows = shocks.shape[1]
    width = loadings.shape[1]
    local = width // BLOCK
    trades = netting.shape[1]
    jn = BLOCK // scen_n
    fac = lax.axis_index("fac")
    scen = lax.axis_index("scen")
    z, x = fac // XS, lax.rem(fac, XS)
    y, c = scen // CORES, lax.rem(scen, CORES)

    barrier = pltpu.get_barrier_semaphore()
    partners = 0
    for d in range(1, zs):
        pl.semaphore_signal(
            barrier, inc=1, device_id={"fac": lax.rem(z + d, zs) * XS + x}, device_id_type=MESH
        )
        partners += 1
    for d in range(1, XS):
        pl.semaphore_signal(
            barrier, inc=1, device_id={"fac": z * XS + lax.rem(x + d, XS)}, device_id_type=MESH
        )
        partners += 1
    for d in range(1, scen_n):
        pl.semaphore_signal(
            barrier, inc=1, device_id={"scen": lax.rem(scen + d, scen_n)}, device_id_type=MESH
        )
        partners += 1

    for i in FIRST:
        loads[i].wait()

    dep = deps[...]
    slot = jnp.zeros_like(dep)
    for b in range(place.shape[0]):
        slot = jnp.where(dep == b, place[b], slot)
    keys[x, 0, :, 0:trades] = slot[0:1]
    keys[x, 0, :, trades : 2 * trades] = slot[1:2]
    keys[x, 0, :, 2 * trades : 3 * trades] = netting[...]
    w32[...] = weights[...].astype(F32)
    pick = (
        lax.broadcasted_iota(jnp.int32, (jn, BLOCK), 1)
        == lax.broadcasted_iota(jnp.int32, (jn, BLOCK), 0) + scen * jn
    ).astype(F32).astype(BF16)
    chosen = [
        lax.dot_general(
            pick, w32[pl.ds(k, trades, stride=2), :].astype(BF16), NT, preferred_element_type=F32
        )
        for k in range(2)
    ]
    wg[x, 0] = jnp.concatenate(chosen, axis=0).astype(BF16)

    near = [0]
    for d in range(1, zs // 2 + 1):
        near += [d] if 2 * d == zs else [d, zs - d]
    cut = zs * 5 // 8
    groups = ((0, cut), (cut, zs))

    def z_copy(kind, d):
        buffer = keys if kind == 0 else wg
        return pltpu.make_async_remote_copy(
            src_ref=buffer.at[x, 0],
            dst_ref=buffer.at[x, near.index(d)],
            send_sem=z_send.at[kind, d],
            recv_sem=z_recv.at[kind, d],
            device_id={"fac": lax.rem(z + d, zs) * XS + x},
            device_id_type=MESH,
        )

    def x_copy(kind, d, piece, from_x):
        buffer = keys if kind == 0 else wg
        low, high = groups[piece]
        ref = buffer.at[from_x, pl.ds(low, high - low)]
        return pltpu.make_async_remote_copy(
            src_ref=ref,
            dst_ref=ref,
            send_sem=x_send.at[kind, d, piece],
            recv_sem=x_recv.at[kind, d, piece],
            device_id={"fac": z * XS + lax.rem(x + d, XS)},
            device_id_type=MESH,
        )

    pl.semaphore_wait(barrier, partners)
    for d in near[:0:-1]:
        for kind in range(2):
            z_copy(kind, d).start()
    for i in LATER:
        loads[i].wait()

    p_rings = []
    cut_rows = rows // P_CUTS
    for date in range(DATES):

        def p_view(owner, piece, date=date):
            return pg.at[date, owner, pl.ds(piece * cut_rows, cut_rows)]

        p_rings.append(
            Ring(
                zs,
                z,
                "fac",
                lambda i: i * XS + x,
                p_view,
                p_send.at[date],
                p_recv.at[date],
                P_CUTS,
                (0, 1, 1, 1, 1),
            )
        )

    col_q = lax.broadcasted_iota(jnp.int32, (width, width), 1)
    col_f = (
        lax.rem(lax.div(col_q, jn), local) * BLOCK
        + lax.div(col_q, jn * local) * jn
        + lax.rem(col_q, jn)
    )
    perm = (lax.broadcasted_iota(jnp.int32, (width, width), 0) == col_f).astype(F32).astype(BF16)
    v = vol[...]
    drift = 0.5 * v * v
    for date in range(DATES):
        diffuse = jnp.dot(shocks[date], loadings[...], preferred_element_type=F32)
        number = counts[date].astype(F32)
        change = (
            v * diffuse
            - drift
            + number * jump_mean[...]
            + jnp.sqrt(number) * jump_vol[...] * noise[date].astype(F32)
        )
        now = change if date == 0 else level[...] + change
        if date < DATES - 1:
            level[...] = now
        prices = (jnp.exp(now) - 1.0).astype(BF16)
        pg[date, z] = jnp.dot(prices, perm, preferred_element_type=F32).astype(BF16)
        p_rings[date].begin()

    sets = XS * SETS
    macc[...] = jnp.zeros_like(macc)

    def form(owner, piece):
        low, high = groups[piece]

        @pl.loop(low, high)
        def _(at):
            columns = pl.ds(pl.multiple_of(at * trades, trades), trades)
            key = keys[owner, at]
            line = key[:, 2 * trades : 3 * trades] - sets * z
            marks[:, columns] = jnp.where(
                lax.broadcasted_iota(jnp.int32, (sets, trades), 0) == line, 1.0, 0.0
            ).astype(BF16)
            w = wg[owner, at].astype(F32)
            w0, w1 = w[0:jn], w[jn : 2 * jn]
            first = key[:, 0:trades] - local * x
            second = key[:, trades : 2 * trades] - local * x
            spread[:, columns] = jnp.concatenate(
                [
                    jnp.where(first == b, w0, 0.0) + jnp.where(second == b, w1, 0.0)
                    for b in [
                        to_z * XS * local + of for to_z in range(zs) for of in range(local)
                    ]
                ],
                axis=0,
            ).astype(BF16)

        columns = pl.ds(low * trades, (high - low) * trades)
        macc[...] += lax.dot_general(
            spread[:, columns], marks[:, columns], NT, preferred_element_type=F32
        )

    def form_from(d, piece):
        from_x = lax.rem(x - d + XS, XS)
        for kind in range(2):
            x_copy(kind, d, piece, from_x).wait_recv()
        form(from_x, piece)

    for piece, (low, high) in enumerate(groups):
        for d in near[max(low, 1) : high]:
            for kind in range(2):
                z_copy(kind, d).wait_recv()
        for d in (2, 1, XS - 1):
            for kind in range(2):
                x_copy(kind, d, piece, x).start()
        if piece == 1:
            p_rings[0].step(1)
        form(x, piece)
    form_from(1, 0)
    form_from(XS - 1, 0)
    form_from(2, 0)
    p_rings[1].step(1)
    form_from(1, 1)
    form_from(XS - 1, 1)
    form_from(2, 1)
    mg[scen] = macc[...].astype(BF16)

    cut_tall = macc.shape[0] // M_CUTS

    def m_view(core):
        def view(owner, piece):
            return mg.at[owner * CORES + core, pl.ds(piece * cut_tall, cut_tall)]

        return view

    m_ring = Ring(
        ys,
        y,
        "scen",
        lambda i: i * CORES + c,
        m_view(c),
        m_send,
        m_recv,
        M_CUTS,
        (0, 1, 2, 1, 2),
    )
    other = 1 - c

    def c_copy(way, d, piece, core):
        ref = m_view(core)(m_ring.owner(way, d), piece)
        return pltpu.make_async_remote_copy(
            src_ref=ref,
            dst_ref=ref,
            send_sem=c_send.at[way, d, piece],
            recv_sem=c_recv.at[way, d, piece],
            device_id={"scen": y * CORES + other},
            device_id_type=MESH,
        )

    def pass_on(way, d, piece):
        c_copy(way, d, piece, c).start()

    c_pieces = [(0, 0, piece) for piece in range(M_CUTS)] + [
        (way, d, piece)
        for d in range(1, ys // 2 + 1)
        for way in range(2)
        for piece in m_ring.pieces(way, d)
    ]
    m_ring.begin()
    for piece in range(M_CUTS):
        pass_on(0, 0, piece)
    p_rings[0].step(2)
    p_rings[1].step(2)
    m_ring.step(2, pass_on)
    p_rings[0].step(3)
    m_ring.step(1, pass_on)
    p_rings[1].step(3)
    m_ring.step(3, pass_on)
    m_ring.step(4, pass_on)
    for way, d, piece in c_pieces:
        c_copy(way, d, piece, other).wait_recv()

    def r_copy(date, d, slot_at):
        return pltpu.make_async_remote_copy(
            src_ref=part.at[date, slot_at],
            dst_ref=back.at[date, d],
            send_sem=r_send.at[date, d],
            recv_sem=r_recv.at[date, d],
            device_id={"fac": z * XS + lax.rem(x + d, XS)},
            device_id_type=MESH,
        )

    tall = local * jn
    for date in range(DATES):
        p_rings[date].step(4)
        total = None
        for at in range(zs):
            term = jnp.dot(
                pg[date, at],
                mg[:, at * tall : (at + 1) * tall, :].reshape(scen_n * tall, sets),
                preferred_element_type=F32,
            )
            total = term if total is None else total + term
        turned = total.T.reshape(XS, SETS, rows)
        nets[date] = turned
        part[date] = turned.astype(BF16)
        for d in (1, XS - 1, 2):
            r_copy(date, d, lax.rem(x + d, XS)).start()
    for date in range(DATES):
        total = nets[date, x]
        for d in (1, XS - 1, 2):
            r_copy(date, d, 0).wait_recv()
            total = total + back[date, d].astype(F32)
        expo[date] = jnp.maximum(total, 0.0)

    both = jnp.concatenate([expo[date] for date in range(DATES)], axis=0)
    high = both.astype(BF16)
    low = (both - high.astype(F32)).astype(BF16)
    row = lax.dot_general(
        jnp.ones((8, 2 * rows), BF16),
        jnp.concatenate([high, low], axis=1),
        NT,
        preferred_element_type=F32,
    )
    sums[0] = row[0:1]

    def s_copy(d):
        return pltpu.make_async_remote_copy(
            src_ref=sums.at[0],
            dst_ref=sums.at[d],
            send_sem=s_send.at[d],
            recv_sem=s_recv.at[d],
            device_id={"scen": lax.rem(scen + d, scen_n)},
            device_id_type=MESH,
        )

    for d in sorted(range(1, scen_n), key=lambda d: -min(d, scen_n - d)):
        s_copy(d).start()
    for kind in range(2):
        for d in range(1, zs):
            z_copy(kind, d).wait_send()
        for d in range(1, XS):
            for piece in range(2):
                x_copy(kind, d, piece, x).wait_send()
    for ring in p_rings:
        ring.sent()
    m_ring.sent()
    for way, d, piece in c_pieces:
        c_copy(way, d, piece, c).wait_send()
    for date in range(DATES):
        for d in range(1, XS):
            r_copy(date, d, 0).wait_send()
    for d in range(1, scen_n):
        s_copy(d).wait_recv()
    average = jnp.sum(sums[...], axis=0) / (rows * scen_n)
    for date in range(DATES):
        mean[date : date + 1, :] = average[:, date * SETS : (date + 1) * SETS]

    for d in range(1, scen_n):
        s_copy(d).wait_send()


def body(
    shocks,
    loadings,
    vol,
    jump_counts,
    jump_noise,
    jump_mean,
    jump_vol,
    dependencies,
    block_slot,
    trade_weights,
    netting,
):
    fac_n = lax.axis_size("fac")
    scen_n = lax.axis_size("scen")
    zs = fac_n // XS
    ys = scen_n // CORES
    rows = shocks.shape[1]
    width = loadings.shape[1]
    trades = netting.shape[0]
    local = width // BLOCK
    jn = BLOCK // scen_n
    tall = zs * local * jn
    sets = XS * SETS
    vmem = pl.BlockSpec(memory_space=pltpu.VMEM)
    hbm = pl.BlockSpec(memory_space=pltpu.HBM)
    dma = pltpu.SemaphoreType.DMA
    arrays = (
        shocks,
        loadings,
        vol.reshape(1, width),
        jump_counts,
        jump_noise,
        jump_mean.reshape(1, width),
        jump_vol.reshape(1, width),
        dependencies.T,
        block_slot,
        trade_weights.reshape(2 * trades, BLOCK),
        netting.reshape(1, trades),
    )
    return pl.pallas_call(
        functools.partial(kernel, fac_n, scen_n),
        out_shape=(
            jax.ShapeDtypeStruct((DATES, SETS, rows), F32),
            jax.ShapeDtypeStruct((DATES, SETS), F32),
        ),
        in_specs=[hbm] * INPUTS,
        out_specs=(vmem, vmem),
        scratch_shapes=[
            (pltpu.SMEM if i == 8 else pltpu.VMEM)(a.shape, a.dtype) for i, a in enumerate(arrays)
        ]
        + [
            dma((INPUTS,)),
            pltpu.VMEM((2 * trades, BLOCK), F32),
            pltpu.VMEM((XS, zs, 1, 3 * trades), jnp.int32),
            pltpu.VMEM((XS, zs, 2 * jn, trades), BF16),
            pltpu.VMEM((sets, zs * trades), BF16),
            pltpu.VMEM((tall, zs * trades), BF16),
            pltpu.VMEM((tall, sets), F32),
            pltpu.VMEM((scen_n, tall, sets), BF16),
            pltpu.VMEM((rows, width), F32),
            pltpu.VMEM((DATES, zs, rows, width), BF16),
            pltpu.VMEM((DATES, XS, SETS, rows), F32),
            pltpu.VMEM((DATES, XS, SETS, rows), BF16),
            pltpu.VMEM((DATES, XS, SETS, rows), BF16),
            pltpu.VMEM((scen_n, 1, DATES * SETS), F32),
            dma((2, zs)),
            dma((2, zs)),
            dma((2, XS, 2)),
            dma((2, XS, 2)),
            dma((DATES, 2, zs // 2 + 1, P_CUTS)),
            dma((DATES, 2, zs // 2 + 1, P_CUTS)),
            dma((2, ys // 2 + 1, M_CUTS)),
            dma((2, ys // 2 + 1, M_CUTS)),
            dma((2, ys // 2 + 1, M_CUTS)),
            dma((2, ys // 2 + 1, M_CUTS)),
            dma((DATES, XS)),
            dma((DATES, XS)),
            dma((scen_n,)),
            dma((scen_n,)),
        ],
        compiler_params=pltpu.CompilerParams(
            collective_id=0, has_side_effects=True, vmem_limit_bytes=55040 * 1024
        ),
    )(*arrays)


def solution(mesh):
    placed = (
        P(None, "scen", None),
        P(None, "fac"),
        P("fac"),
        P(None, "scen", "fac"),
        P(None, "scen", "fac"),
        P("fac"),
        P("fac"),
        P("fac", None),
        P(),
        P("fac", None, None),
        P("fac"),
    )
    return jax.shard_map(
        body,
        mesh=mesh,
        in_specs=placed,
        out_specs=(P(None, "fac", "scen"), P(None, "fac")),
        check_vma=False,
    )
```

```python
import functools

import jax
import jax.numpy as jnp
from jax import lax
from jax.experimental import pallas as pl
from jax.experimental.pallas import tpu as pltpu
from jax.sharding import PartitionSpec as P

BLOCK = 128
SETS = 64
DATES = 2
CORES = 2
XS = 4
P_CUTS = 2
M_CUTS = 2
MESH = pl.DeviceIdType.MESH
F32 = jnp.float32
BF16 = jnp.bfloat16
NT = (((1,), (1,)), ((), ()))
INPUTS = 11
FIRST = (8, 7, 10, 9)
LATER = (0, 1, 3, 4, 2, 5, 6)


class Ring:
    def __init__(self, n, me, axis, device, view, send, recv, cuts, hops):
        self.n, self.me, self.axis, self.device, self.view = n, me, axis, device, view
        self.send, self.recv, self.cuts, self.hops = send, recv, cuts, hops
        self.last = n // 2

    def pieces(self, way, d):
        half = self.cuts // 2
        if d < self.last:
            return range(self.cuts)
        return range(way * half, (way + 1) * half)

    def owner(self, way, d):
        step = -d if way == 0 else d
        return lax.rem(self.me + step + self.n, self.n)

    def copy(self, way, d, piece, shift):
        ref = self.view(self.owner(way, d - shift), piece)
        to = self.owner(way, -self.hops[d])
        return pltpu.make_async_remote_copy(
            src_ref=ref,
            dst_ref=ref,
            send_sem=self.send.at[way, d, piece],
            recv_sem=self.recv.at[way, d, piece],
            device_id={self.axis: self.device(to)},
            device_id_type=MESH,
        )

    def start(self, way, d, piece):
        self.copy(way, d, piece, self.hops[d]).start()

    def begin(self):
        for d in range(self.last, 0, -1):
            for piece in range(self.cuts):
                for way in range(2):
                    if d == self.hops[d] and piece in self.pieces(way, d):
                        self.start(way, d, piece)

    def step(self, d, also=None):
        if d > self.last:
            return
        for piece in range(self.cuts):
            for way in range(2):
                if piece in self.pieces(way, d):
                    self.copy(way, d, piece, 0).wait_recv()
                    for later in range(d + 1, self.last + 1):
                        if later - self.hops[later] == d and piece in self.pieces(way, later):
                            self.start(way, later, piece)
                    if also is not None:
                        also(way, d, piece)

    def sent(self):
        for d in range(1, self.last + 1):
            for way in range(2):
                for piece in self.pieces(way, d):
                    self.copy(way, d, piece, self.hops[d]).wait_send()


def kernel(
    fac_n,
    scen_n,
    *refs,
):
    given, refs = refs[:INPUTS], refs[INPUTS:]
    expo, mean, *refs = refs
    held, refs = refs[:INPUTS], refs[INPUTS:]
    run(fac_n, scen_n, given, held, expo, mean, *refs)


def run(
    fac_n,
    scen_n,
    given,
    held,
    expo,
    mean,
    load_sem,
    w32,
    keys,
    wg,
    marks,
    spread,
    macc,
    mg,
    level,
    pg,
    nets,
    part,
    back,
    sums,
    z_send,
    z_recv,
    x_send,
    x_recv,
    p_send,
    p_recv,
    m_send,
    m_recv,
    c_send,
    c_recv,
    r_send,
    r_recv,
    s_send,
    s_recv,
):
    loads = [
        pltpu.make_async_copy(src, dst, load_sem.at[i])
        for i, (src, dst) in enumerate(zip(given, held))
    ]
    for i in FIRST:
        loads[i].start()
    for i in LATER:
        loads[i].start()
    (shocks, loadings, vol, counts, noise, jump_mean, jump_vol, deps, place, weights, netting) = (
        held
    )
    zs = fac_n // XS
    ys = scen_n // CORES
    rows = shocks.shape[1]
    width = loadings.shape[1]
    local = width // BLOCK
    trades = netting.shape[1]
    jn = BLOCK // scen_n
    fac = lax.axis_index("fac")
    scen = lax.axis_index("scen")
    z, x = fac // XS, lax.rem(fac, XS)
    y, c = scen // CORES, lax.rem(scen, CORES)

    barrier = pltpu.get_barrier_semaphore()
    partners = 0
    for d in range(1, zs):
        pl.semaphore_signal(
            barrier, inc=1, device_id={"fac": lax.rem(z + d, zs) * XS + x}, device_id_type=MESH
        )
        partners += 1
    for d in range(1, XS):
        pl.semaphore_signal(
            barrier, inc=1, device_id={"fac": z * XS + lax.rem(x + d, XS)}, device_id_type=MESH
        )
        partners += 1
    for d in range(1, scen_n):
        pl.semaphore_signal(
            barrier, inc=1, device_id={"scen": lax.rem(scen + d, scen_n)}, device_id_type=MESH
        )
        partners += 1

    for i in FIRST:
        loads[i].wait()

    dep = deps[...]
    slot = jnp.zeros_like(dep)
    for b in range(place.shape[0]):
        slot = jnp.where(dep == b, place[b], slot)
    keys[x, 0, :, 0:trades] = slot[0:1]
    keys[x, 0, :, trades : 2 * trades] = slot[1:2]
    keys[x, 0, :, 2 * trades : 3 * trades] = netting[...]
    w32[...] = weights[...].astype(F32)
    pick = (
        lax.broadcasted_iota(jnp.int32, (jn, BLOCK), 1)
        == lax.broadcasted_iota(jnp.int32, (jn, BLOCK), 0) + scen * jn
    ).astype(F32).astype(BF16)
    chosen = [
        lax.dot_general(
            pick, w32[pl.ds(k, trades, stride=2), :].astype(BF16), NT, preferred_element_type=F32
        )
        for k in range(2)
    ]
    wg[x, 0] = jnp.concatenate(chosen, axis=0).astype(BF16)

    near = [0]
    for d in range(1, zs // 2 + 1):
        near += [d] if 2 * d == zs else [d, zs - d]
    cut = zs * 5 // 8
    groups = ((0, cut), (cut, zs))

    def z_copy(kind, d):
        buffer = keys if kind == 0 else wg
        return pltpu.make_async_remote_copy(
            src_ref=buffer.at[x, 0],
            dst_ref=buffer.at[x, near.index(d)],
            send_sem=z_send.at[kind, d],
            recv_sem=z_recv.at[kind, d],
            device_id={"fac": lax.rem(z + d, zs) * XS + x},
            device_id_type=MESH,
        )

    def x_copy(kind, d, piece, from_x):
        buffer = keys if kind == 0 else wg
        low, high = groups[piece]
        ref = buffer.at[from_x, pl.ds(low, high - low)]
        return pltpu.make_async_remote_copy(
            src_ref=ref,
            dst_ref=ref,
            send_sem=x_send.at[kind, d, piece],
            recv_sem=x_recv.at[kind, d, piece],
            device_id={"fac": z * XS + lax.rem(x + d, XS)},
            device_id_type=MESH,
        )

    col_q = lax.broadcasted_iota(jnp.int32, (width, width), 1)
    col_f = (
        lax.rem(lax.div(col_q, jn), local) * BLOCK
        + lax.div(col_q, jn * local) * jn
        + lax.rem(col_q, jn)
    )
    perm = (lax.broadcasted_iota(jnp.int32, (width, width), 0) == col_f).astype(F32).astype(BF16)
    pl.semaphore_wait(barrier, partners)
    for d in near[:0:-1]:
        for kind in range(2):
            z_copy(kind, d).start()
    for i in LATER:
        loads[i].wait()

    p_rings = []
    cut_rows = rows // P_CUTS
    for date in range(DATES):

        def p_view(owner, piece, date=date):
            return pg.at[date, owner, pl.ds(piece * cut_rows, cut_rows)]

        p_rings.append(
            Ring(
                zs,
                z,
                "fac",
                lambda i: i * XS + x,
                p_view,
                p_send.at[date],
                p_recv.at[date],
                P_CUTS,
                (0, 1, 1, 1, 1),
            )
        )

    v = vol[...]
    drift = 0.5 * v * v
    for date in range(DATES):
        diffuse = jnp.dot(shocks[date], loadings[...], preferred_element_type=F32)
        number = counts[date].astype(F32)
        change = (
            v * diffuse
            - drift
            + number * jump_mean[...]
            + jnp.sqrt(number) * jump_vol[...] * noise[date].astype(F32)
        )
        now = change if date == 0 else level[...] + change
        if date < DATES - 1:
            level[...] = now
        prices = (jnp.exp(now) - 1.0).astype(BF16)
        pg[date, z] = jnp.dot(prices, perm, preferred_element_type=F32).astype(BF16)
        p_rings[date].begin()

    sets = XS * SETS
    macc[...] = jnp.zeros_like(macc)

    def form(owner, piece):
        low, high = groups[piece]

        @pl.loop(low, high)
        def _(at):
            columns = pl.ds(pl.multiple_of(at * trades, trades), trades)
            key = keys[owner, at]
            line = key[:, 2 * trades : 3 * trades] - sets * z
            marks[:, columns] = jnp.where(
                lax.broadcasted_iota(jnp.int32, (sets, trades), 0) == line, 1.0, 0.0
            ).astype(BF16)
            w = wg[owner, at].astype(F32)
            w0, w1 = w[0:jn], w[jn : 2 * jn]
            first = key[:, 0:trades] - local * x
            second = key[:, trades : 2 * trades] - local * x
            spread[:, columns] = jnp.concatenate(
                [
                    jnp.where(first == b, w0, 0.0) + jnp.where(second == b, w1, 0.0)
                    for b in [
                        to_z * XS * local + of for to_z in range(zs) for of in range(local)
                    ]
                ],
                axis=0,
            ).astype(BF16)

        columns = pl.ds(low * trades, (high - low) * trades)
        macc[...] += lax.dot_general(
            spread[:, columns], marks[:, columns], NT, preferred_element_type=F32
        )

    def form_from(d, piece):
        from_x = lax.rem(x - d + XS, XS)
        for kind in range(2):
            x_copy(kind, d, piece, from_x).wait_recv()
        form(from_x, piece)

    for piece, (low, high) in enumerate(groups):
        for d in near[max(low, 1) : high]:
            for kind in range(2):
                z_copy(kind, d).wait_recv()
        for d in (2, 1, XS - 1):
            for kind in range(2):
                x_copy(kind, d, piece, x).start()
        if piece == 1:
            p_rings[0].step(1)
        form(x, piece)
    form_from(1, 0)
    form_from(XS - 1, 0)
    form_from(2, 0)
    p_rings[1].step(1)
    form_from(1, 1)
    form_from(XS - 1, 1)
    form_from(2, 1)
    mg[scen] = macc[...].astype(BF16)

    cut_tall = macc.shape[0] // M_CUTS

    def m_view(core):
        def view(owner, piece):
            return mg.at[owner * CORES + core, pl.ds(piece * cut_tall, cut_tall)]

        return view

    m_ring = Ring(
        ys,
        y,
        "scen",
        lambda i: i * CORES + c,
        m_view(c),
        m_send,
        m_recv,
        M_CUTS,
        (0, 1, 2, 1, 2),
    )
    other = 1 - c

    def c_copy(way, d, piece, core):
        ref = m_view(core)(m_ring.owner(way, d), piece)
        return pltpu.make_async_remote_copy(
            src_ref=ref,
            dst_ref=ref,
            send_sem=c_send.at[way, d, piece],
            recv_sem=c_recv.at[way, d, piece],
            device_id={"scen": y * CORES + other},
            device_id_type=MESH,
        )

    def pass_on(way, d, piece):
        c_copy(way, d, piece, c).start()

    c_pieces = [(0, 0, piece) for piece in range(M_CUTS)] + [
        (way, d, piece)
        for d in range(1, ys // 2 + 1)
        for way in range(2)
        for piece in m_ring.pieces(way, d)
    ]
    m_ring.begin()
    for piece in range(M_CUTS):
        pass_on(0, 0, piece)
    p_rings[0].step(2)
    p_rings[1].step(2)
    m_ring.step(2, pass_on)
    p_rings[0].step(3)
    m_ring.step(1, pass_on)
    p_rings[1].step(3)
    m_ring.step(3, pass_on)
    m_ring.step(4, pass_on)
    for way, d, piece in c_pieces:
        c_copy(way, d, piece, other).wait_recv()

    def r_copy(date, d, slot_at):
        return pltpu.make_async_remote_copy(
            src_ref=part.at[date, slot_at],
            dst_ref=back.at[date, d],
            send_sem=r_send.at[date, d],
            recv_sem=r_recv.at[date, d],
            device_id={"fac": z * XS + lax.rem(x + d, XS)},
            device_id_type=MESH,
        )

    tall = local * jn
    for date in range(DATES):
        p_rings[date].step(4)
        total = None
        for at in range(zs):
            term = jnp.dot(
                pg[date, at],
                mg[:, at * tall : (at + 1) * tall, :].reshape(scen_n * tall, sets),
                preferred_element_type=F32,
            )
            total = term if total is None else total + term
        turned = total.T.reshape(XS, SETS, rows)
        nets[date] = turned
        part[date] = turned.astype(BF16)
        for d in (1, XS - 1, 2):
            r_copy(date, d, lax.rem(x + d, XS)).start()
    totals = []
    for date in range(DATES):
        total = nets[date, x]
        for d in (1, XS - 1, 2):
            r_copy(date, d, 0).wait_recv()
            total = total + back[date, d].astype(F32)
        total = jnp.maximum(total, 0.0)
        expo[date] = total
        high = total.astype(BF16)
        low = (total - high.astype(F32)).astype(BF16)
        row = lax.dot_general(
            jnp.ones((8, 2 * rows), BF16),
            jnp.concatenate([high, low], axis=1),
            NT,
            preferred_element_type=F32,
        )
        totals.append(row[0:1])

    sums[0] = jnp.concatenate(totals, axis=1)

    def s_copy(d):
        return pltpu.make_async_remote_copy(
            src_ref=sums.at[0],
            dst_ref=sums.at[d],
            send_sem=s_send.at[d],
            recv_sem=s_recv.at[d],
            device_id={"scen": lax.rem(scen + d, scen_n)},
            device_id_type=MESH,
        )

    for d in sorted(range(1, scen_n), key=lambda d: -min(d, scen_n - d)):
        s_copy(d).start()
    for kind in range(2):
        for d in range(1, zs):
            z_copy(kind, d).wait_send()
        for d in range(1, XS):
            for piece in range(2):
                x_copy(kind, d, piece, x).wait_send()
    for ring in p_rings:
        ring.sent()
    m_ring.sent()
    for way, d, piece in c_pieces:
        c_copy(way, d, piece, c).wait_send()
    for date in range(DATES):
        for d in range(1, XS):
            r_copy(date, d, 0).wait_send()
    for d in range(1, scen_n):
        s_copy(d).wait_recv()
    average = jnp.sum(sums[...], axis=0) / (rows * scen_n)
    for date in range(DATES):
        mean[date : date + 1, :] = average[:, date * SETS : (date + 1) * SETS]

    for d in range(1, scen_n):
        s_copy(d).wait_send()


def body(
    shocks,
    loadings,
    vol,
    jump_counts,
    jump_noise,
    jump_mean,
    jump_vol,
    dependencies,
    block_slot,
    trade_weights,
    netting,
):
    fac_n = lax.axis_size("fac")
    scen_n = lax.axis_size("scen")
    zs = fac_n // XS
    ys = scen_n // CORES
    rows = shocks.shape[1]
    width = loadings.shape[1]
    trades = netting.shape[0]
    local = width // BLOCK
    jn = BLOCK // scen_n
    tall = zs * local * jn
    sets = XS * SETS
    vmem = pl.BlockSpec(memory_space=pltpu.VMEM)
    hbm = pl.BlockSpec(memory_space=pltpu.HBM)
    dma = pltpu.SemaphoreType.DMA
    arrays = (
        shocks,
        loadings,
        vol.reshape(1, width),
        jump_counts,
        jump_noise,
        jump_mean.reshape(1, width),
        jump_vol.reshape(1, width),
        dependencies.T,
        block_slot,
        trade_weights.reshape(2 * trades, BLOCK),
        netting.reshape(1, trades),
    )
    return pl.pallas_call(
        functools.partial(kernel, fac_n, scen_n),
        out_shape=(
            jax.ShapeDtypeStruct((DATES, SETS, rows), F32),
            jax.ShapeDtypeStruct((DATES, SETS), F32),
        ),
        in_specs=[hbm] * INPUTS,
        out_specs=(vmem, vmem),
        scratch_shapes=[
            (pltpu.SMEM if i == 8 else pltpu.VMEM)(a.shape, a.dtype) for i, a in enumerate(arrays)
        ]
        + [
            dma((INPUTS,)),
            pltpu.VMEM((2 * trades, BLOCK), F32),
            pltpu.VMEM((XS, zs, 1, 3 * trades), jnp.int32),
            pltpu.VMEM((XS, zs, 2 * jn, trades), BF16),
            pltpu.VMEM((sets, zs * trades), BF16),
            pltpu.VMEM((tall, zs * trades), BF16),
            pltpu.VMEM((tall, sets), F32),
            pltpu.VMEM((scen_n, tall, sets), BF16),
            pltpu.VMEM((rows, width), F32),
            pltpu.VMEM((DATES, zs, rows, width), BF16),
            pltpu.VMEM((DATES, XS, SETS, rows), F32),
            pltpu.VMEM((DATES, XS, SETS, rows), BF16),
            pltpu.VMEM((DATES, XS, SETS, rows), BF16),
            pltpu.VMEM((scen_n, 1, DATES * SETS), F32),
            dma((2, zs)),
            dma((2, zs)),
            dma((2, XS, 2)),
            dma((2, XS, 2)),
            dma((DATES, 2, zs // 2 + 1, P_CUTS)),
            dma((DATES, 2, zs // 2 + 1, P_CUTS)),
            dma((2, ys // 2 + 1, M_CUTS)),
            dma((2, ys // 2 + 1, M_CUTS)),
            dma((2, ys // 2 + 1, M_CUTS)),
            dma((2, ys // 2 + 1, M_CUTS)),
            dma((DATES, XS)),
            dma((DATES, XS)),
            dma((scen_n,)),
            dma((scen_n,)),
        ],
        compiler_params=pltpu.CompilerParams(
            collective_id=0, has_side_effects=True, vmem_limit_bytes=55040 * 1024
        ),
    )(*arrays)


def solution(mesh):
    placed = (
        P(None, "scen", None),
        P(None, "fac"),
        P("fac"),
        P(None, "scen", "fac"),
        P(None, "scen", "fac"),
        P("fac"),
        P("fac"),
        P("fac", None),
        P(),
        P("fac", None, None),
        P("fac"),
    )
    return jax.shard_map(
        body,
        mesh=mesh,
        in_specs=placed,
        out_specs=(P(None, "fac", "scen"), P(None, "fac")),
        check_vma=False,
    )
```
